512 devices in a mesh: lev: 4 (over y), tile: 64 (over z_lo, x, core), sec: 2 (over z_hi).
Axes of the slice: x: 4, y: 4, z: 16 (z_hi: 2, z_lo: 8; z = z_hi * 8 + z_lo), core: 2. Of those that a mesh axis runs over, the one named last changes fastest.
Arguments:
- fields: float32 [3, 64, 4, 128, 360], P(None, ('lev', 'sec'), None, 'tile'), may hold values from -6 to 6
- surface: float32 [4, 128, 360], P(None, 'tile'), may hold values from -6 to 6
- cot_fields: float32 [3, 64, 4, 128, 360], P(None, ('lev', 'sec'), None, 'tile'), may hold values from -6 to 6
- cot_surface: float32 [4, 128, 360], P(None, 'tile'), may hold values from -6 to 6
- land_sea: int32 [128, 360], P('tile'), may hold values 0 or 1
- w_in: bfloat16 [192, 384], replicated, may hold values from -0.4375 to 0.4375
- w_mid: bfloat16 [384, 384], replicated, may hold values from -0.3125 to 0.3125
- w_out: bfloat16 [384, 192], replicated, may hold values from -0.3125 to 0.3125
- bias_in: float32 [2, 384], replicated, may hold values from -4 to 4
Outputs:
- final_fields: float32 [3, 64, 4, 128, 360], P(None, ('lev', 'sec'), None, 'tile')
- final_surface: float32 [4, 128, 360], P(None, 'tile')
- fields_grad: float32 [3, 64, 4, 128, 360], P(None, ('lev', 'sec'), None, 'tile')
- surface_grad: float32 [4, 128, 360], P(None, 'tile')
- w_in_grad: float32 [192, 384], replicated
- w_mid_grad: float32 [384, 384], replicated
- w_out_grad: float32 [384, 192], replicated
- bias_grad: float32 [2, 384], replicated
The draws below stay inside these ranges and needn't reach their ends.
Inputs may be any that keep to these rules, and one draw needn't show every extreme that they name: `land_sea`: 1 marks land, 0 sea.
All inputs are finite; a program needn't handle non-finite values. No bound on the sum of `land_sea` on one device may be relied on, other than what follows from the above.
Results may differ from the reference program's by a relative error of at most 0.005.
Values may be sent and summed in bfloat16 or wider, within the bound.
A program may use at most 64 MiB of HBM per device.

```python
import math
import jax
import jax.numpy as jnp
from jax import lax

NLEV = 64
NLON = 360
HID = 384
STEPS = 2
BATCH = 4
FEAT = 192
NLAT = 128


def with_ends(entries, stream_key, low, largest):
    longest = entries.shape.index(max(entries.shape))
    spots = []
    for shift in (0, 1):
        where = [jax.random.randint(jax.random.fold_in(stream_key, axis), (), 0, length) for axis, length in enumerate(entries.shape)]
        where[longest] = (where[longest] + shift) % entries.shape[longest]
        spots.append(tuple(where))
    return entries.at[spots[0]].set(low).at[spots[1]].set(largest)


def block_scale(own_key, dims, split, least, largest):
    gain = 1.0
    for position, shards_of in split:
        draws = jax.random.uniform(jax.random.fold_in(jax.random.fold_in(own_key, 6), position), (shards_of,), jnp.float32, least / len(split), largest / len(split))
        gain = gain * jnp.repeat(jnp.exp(draws), dims[position] // shards_of).reshape((-1,) + (1,) * (len(dims) - 1 - position))
    return gain


def centred(rng, extent, scale, bound, shards=(), held_as=jnp.bfloat16):
    array = scale * jax.random.normal(rng, extent, jnp.float32)
    if shards:
        array = array * block_scale(rng, extent, shards, -0.22, 0.18)
    return jnp.clip(array, -bound, bound).astype(held_as)


def setup_inputs(seed: int = 0) -> dict:
    arg_keys = jax.random.split(jax.random.key(seed), 10)
    return {
        "fields": centred(arg_keys[0], (3, NLEV, BATCH, NLAT, NLON), 1.0, 6.0, ((1, 8), (3, 64)), jnp.float32),
        "surface": centred(arg_keys[1], (BATCH, NLAT, NLON), 1.0, 6.0, ((1, 64),), jnp.float32),
        "cot_fields": centred(arg_keys[2], (3, NLEV, BATCH, NLAT, NLON), 1.0, 6.0, ((1, 8), (3, 64)), jnp.float32),
        "cot_surface": centred(arg_keys[3], (BATCH, NLAT, NLON), 1.0, 6.0, ((1, 64),), jnp.float32),
        "land_sea": with_ends((jax.random.randint(arg_keys[4], (NLAT, NLON), 0, 10) < 3).astype(jnp.int32), jax.random.fold_in(arg_keys[4], 1), 0, 1),
        "w_in": centred(arg_keys[5], (FEAT, HID), FEAT ** -0.5, 0.4375),
        "w_mid": centred(arg_keys[6], (HID, HID), HID ** -0.5, 0.3125),
        "w_out": centred(arg_keys[7], (HID, FEAT), HID ** -0.5, 0.3125),
        "bias_in": centred(arg_keys[8], (2, HID), 1.0, 4.0, (), jnp.float32),
    }


TIME_STEP = 0.1
COS_FLOOR = 0.2
INV_SQRT_TWO = 1.0 / math.sqrt(2.0)
INV_SQRT_TWO_PI = 1.0 / math.sqrt(2.0 * math.pi)

def gelu_slope(values):
    cumulative = 0.5 * (1.0 + lax.erf(values * INV_SQRT_TWO))
    density = jnp.exp(-0.5 * values * values) * INV_SQRT_TWO_PI
    return cumulative + values * density

def lon_change(values, x_factor):
    return (jnp.roll(values, -1, axis=-1) - jnp.roll(values, 1, axis=-1)) * x_factor

def lat_change(values):
    padded = jnp.pad(values, ((0, 0), (0, 0), (1, 1), (0, 0)))
    return (padded[:, :, 2:, :] - padded[:, :, :-2, :]) * 0.5

def rising_sum(values):
    return jnp.cumsum(values, axis=0)

def column_prefix_accumulation(values):
    return jnp.flip(jnp.cumsum(jnp.flip(values, 0), axis=0), 0)

def dynamics(current_fields_bundle, current_ground_pressure, x_factor, sin_lat, layer_thickness_fraction):
    zonal_velocity, meridional_velocity, thermal_field = (current_fields_bundle[0], current_fields_bundle[1], current_fields_bundle[2])
    velocity_spreading = lon_change(zonal_velocity, x_factor) + lat_change(meridional_velocity)
    mass_flux = rising_sum(velocity_spreading) / NLEV
    column_total = lax.optimization_barrier(jnp.sum(velocity_spreading, axis=0))
    gravity_potential_elevation = column_prefix_accumulation(layer_thickness_fraction * thermal_field) + current_ground_pressure[None]
    zonal_tend = -lon_change(gravity_potential_elevation, x_factor) + sin_lat * meridional_velocity
    merid_tend = -lat_change(gravity_potential_elevation) - sin_lat * zonal_velocity
    temp_tend = -mass_flux
    return (jnp.stack([zonal_tend, merid_tend, temp_tend]), -column_total / NLEV)

def adjoint(field_bar, surface_bar, x_factor, sin_lat, layer_thickness_fraction):
    a_zonal, a_merid, a_temp = (field_bar[0], field_bar[1], field_bar[2])
    height_bar = lon_change(a_zonal, x_factor) + lat_change(a_merid)
    temp_bar = layer_thickness_fraction * rising_sum(height_bar)
    surf_adj = lax.optimization_barrier(jnp.sum(height_bar, axis=0))
    div_bar = (-column_prefix_accumulation(a_temp) - surface_bar[None]) / NLEV
    zonal_bar = -lon_change(div_bar, x_factor) - sin_lat * a_merid
    merid_bar = -lat_change(div_bar) + sin_lat * a_zonal
    return (jnp.stack([zonal_bar, merid_bar, temp_bar]), surf_adj)

def reference(fields, surface, cot_fields, cot_surface, land_sea, w_in, w_mid, w_out, bias_in):
    row_ids = jnp.arange(NLAT).astype(jnp.float32)
    latitude = -0.5 * math.pi + (row_ids + 0.5) * (math.pi / NLAT)
    x_factor = (0.5 / jnp.maximum(jnp.cos(latitude), COS_FLOOR))[:, None]
    sin_lat = jnp.sin(latitude)[:, None]
    level_ids = jnp.arange(NLEV).astype(jnp.float32)
    layer_thickness_fraction = (1.0 / (level_ids + 1.0))[:, None, None, None]
    mask_cols = land_sea.reshape(-1)
    bias_cols = jnp.where(mask_cols[None, :] > 0, bias_in[1][:, None], bias_in[0][:, None])
    land_cols = (mask_cols > 0)[None, :]
    col_total = NLAT * NLON

    def to_cols(values):
        return values.reshape(FEAT, BATCH, col_total).transpose(1, 0, 2)

    def from_cols(values):
        return values.transpose(1, 0, 2).reshape(3, NLEV, BATCH, NLAT, NLON)

    def hidden_layers(x_cols):
        first_pre = jnp.dot(w_in.T, x_cols, preferred_element_type=jnp.float32) + bias_cols
        first_act = jax.nn.gelu(first_pre, approximate=False).astype(jnp.bfloat16)
        second_pre = jnp.dot(w_mid.T, first_act, preferred_element_type=jnp.float32)
        second_act = jax.nn.gelu(second_pre, approximate=False).astype(jnp.bfloat16)
        return (first_pre, first_act, second_pre, second_act)

    def forward_columns(x_cols):
        first_pre, first_act, second_pre, second_act = hidden_layers(x_cols)
        return jnp.dot(w_out.T, second_act, preferred_element_type=jnp.float32).astype(jnp.bfloat16)

    def backward_columns(totals_in, column_pair):
        x_cols, tend_bar = column_pair
        first_pre, first_act, second_pre, second_act = hidden_layers(x_cols)
        second_bar = (jnp.dot(w_out, tend_bar, preferred_element_type=jnp.float32) * gelu_slope(second_pre)).astype(jnp.bfloat16)
        first_bar = (jnp.dot(w_mid, second_bar, preferred_element_type=jnp.float32) * gelu_slope(first_pre)).astype(jnp.bfloat16)
        input_bar = jnp.dot(w_in, first_bar, preferred_element_type=jnp.float32).astype(jnp.bfloat16)
        grad_in = totals_in[0] + jnp.dot(x_cols, first_bar.T, preferred_element_type=jnp.float32)
        grad_mid = totals_in[1] + jnp.dot(first_act, second_bar.T, preferred_element_type=jnp.float32)
        grad_out = totals_in[2] + jnp.dot(second_act, tend_bar.T, preferred_element_type=jnp.float32)
        first_wide = first_bar.astype(jnp.float32)
        zero_f = jnp.zeros((), jnp.float32)
        sea_part = lax.optimization_barrier(jnp.sum(jnp.where(land_cols, zero_f, first_wide), axis=1))
        land_part = lax.optimization_barrier(jnp.sum(jnp.where(land_cols, first_wide, zero_f), axis=1))
        grad_bias = totals_in[3] + jnp.stack([sea_part, land_part])
        return ((grad_in, grad_mid, grad_out, grad_bias), input_bar)
    current_fields_bundle, current_ground_pressure = (fields, surface)
    inputs = []
    for instant in range(STEPS):
        x_all = to_cols(current_fields_bundle.astype(jnp.bfloat16))
        inputs.append(x_all)
        tendency = from_cols(lax.map(forward_columns, x_all)).astype(jnp.float32)
        dyn_fields, dyn_surface = dynamics(current_fields_bundle, current_ground_pressure, x_factor, sin_lat, layer_thickness_fraction)
        current_fields_bundle = current_fields_bundle + TIME_STEP * (dyn_fields + tendency)
        current_ground_pressure = current_ground_pressure + TIME_STEP * dyn_surface
    field_bar, surface_bar = (cot_fields, cot_surface)
    gradient = (jnp.zeros((FEAT, HID), jnp.float32), jnp.zeros((HID, HID), jnp.float32), jnp.zeros((HID, FEAT), jnp.float32), jnp.zeros((2, HID), jnp.float32))
    for instant in reversed(range(STEPS)):
        tend_cols = to_cols((TIME_STEP * field_bar).astype(jnp.bfloat16))
        gradient, input_bar = lax.scan(backward_columns, gradient, (inputs[instant], tend_cols))
        input_levels = from_cols(input_bar).astype(jnp.float32)
        adj_fields, adj_surface = adjoint(field_bar, surface_bar, x_factor, sin_lat, layer_thickness_fraction)
        field_bar = field_bar + TIME_STEP * adj_fields + input_levels
        surface_bar = surface_bar + TIME_STEP * adj_surface
    return (current_fields_bundle, current_ground_pressure, field_bar, surface_bar, gradient[0], gradient[1], gradient[2], gradient[3])
```

```python
import math

import jax
import jax.numpy as jnp
from jax import lax
from jax.sharding import PartitionSpec as P

TIME_STEP = 0.1
COS_FLOOR = 0.2
INV_SQRT_TWO = 1.0 / math.sqrt(2.0)
INV_SQRT_TWO_PI = 1.0 / math.sqrt(2.0 * math.pi)
GROUP = ("lev", "sec")
EVERY = ("lev", "tile", "sec")
HIGH = lax.Precision.HIGHEST


def gelu_parts(values):
    cumulative = 0.5 * (1.0 + lax.erf(values * INV_SQRT_TWO))
    density = jnp.exp(-0.5 * values * values) * INV_SQRT_TWO_PI
    return (values * cumulative).astype(jnp.bfloat16), cumulative + values * density


def dot(a, b):
    return jnp.dot(a, b, preferred_element_type=jnp.float32)


def dot_t(a, b):
    return jnp.einsum("ac,bc->ab", a, b, preferred_element_type=jnp.float32)


def on_device(fields, surface, cot_fields, cot_surface, land_sea, w_in, w_mid, w_out, bias_in):
    nlev = 64
    tiles = lax.axis_size("tile")
    lev_i, tile_i, sec_i = (lax.axis_index(a) for a in EVERY)
    row_in_band = lax.rem(lev_i, 2)
    sample = lax.div(lev_i, 2) * 2 + sec_i
    row = tile_i * 2 + row_in_band
    rows = tiles * 2
    latitude = -0.5 * math.pi + (row.astype(jnp.float32) + 0.5) * (math.pi / rows)
    x_factor = 0.5 / jnp.maximum(jnp.cos(latitude), COS_FLOOR)
    sin_lat = jnp.sin(latitude)
    level = jnp.arange(nlev)
    weight = (1.0 / (level.astype(jnp.float32) + 1.0))[:, None]
    below = (level[:, None] >= level[None, :]).astype(jnp.float32)
    mask = land_sea[row_in_band] > 0
    bias_cols = jnp.where(mask[None, :], bias_in[1][:, None], bias_in[0][:, None])

    def device_of(r, bh, bl):
        return ((bh * 2 + r % 2) * tiles + r // 2) * 2 + bl

    up = [(device_of(r, h, l), device_of(r + 1, h, l)) for r in range(rows - 1) for h in (0, 1) for l in (0, 1)]
    down = [(j, i) for i, j in up]

    def halo(values):
        values = values.astype(jnp.bfloat16)
        before = lax.ppermute(values, EVERY, up).astype(jnp.float32)
        after = lax.ppermute(values, EVERY, down).astype(jnp.float32)
        return (after - before) * 0.5

    def dx(values):
        return (jnp.roll(values, -1, axis=-1) - jnp.roll(values, 1, axis=-1)) * x_factor

    def rising(values):
        return jnp.dot(below, values, precision=HIGH)

    def falling(values):
        return jnp.dot(below.T, values, precision=HIGH)

    def to_columns(values):
        split = values.reshape(3, 8, 2, 2, 2, 360)
        return split.transpose(2, 4, 3, 0, 1, 5).reshape(8, 24, 360).astype(jnp.bfloat16)

    sent = jnp.concatenate([to_columns(fields), to_columns(TIME_STEP * cot_fields)], axis=1)
    arrived = lax.all_to_all(sent, GROUP, split_axis=0, concat_axis=0, tiled=True)
    both = arrived.reshape(8, 2, 3, 8, 360).transpose(1, 2, 0, 3, 4)
    x0 = both[0].reshape(192, 360)
    t0 = both[1].reshape(192, 360)

    def mlp(x):
        first_act, first_slope = gelu_parts(dot(w_in.T, x) + bias_cols)
        second_act, second_slope = gelu_parts(dot(w_mid.T, first_act))
        tendency = dot(w_out.T, second_act).astype(jnp.bfloat16)
        return tendency, (first_act, first_slope, second_act, second_slope)

    def mlp_back(x, tend_bar, kept):
        first_act, first_slope, second_act, second_slope = kept
        second_bar = (dot(w_out, tend_bar) * second_slope).astype(jnp.bfloat16)
        first_bar = (dot(w_mid, second_bar) * first_slope).astype(jnp.bfloat16)
        input_bar = dot(w_in, first_bar).astype(jnp.bfloat16)
        wide = first_bar.astype(jnp.float32)
        zero = jnp.zeros((), jnp.float32)
        grads = (
            dot_t(x, first_bar),
            dot_t(first_act, second_bar),
            dot_t(second_act, tend_bar),
            jnp.stack([jnp.sum(jnp.where(mask, zero, wide), 1), jnp.sum(jnp.where(mask, wide, zero), 1)]),
        )
        return input_bar.astype(jnp.float32), grads

    def dynamics(state, surf, halos):
        u, v = state[:64], state[64:128]
        dv, dh = halos[:64], halos[64:]
        height = falling(weight * state[128:]) + surf
        div = dx(u) + dv
        flux = rising(div) / nlev
        change = jnp.concatenate([-dx(height) + sin_lat * v, -dh - sin_lat * u, -flux])
        return change, -jnp.sum(div, 0) / nlev

    def forward_halo(state, surf):
        return jnp.concatenate([state[64:128], falling(weight * state[128:]) + surf])

    def div_bar(bar, surf_bar):
        return (-falling(bar[128:]) - surf_bar) / nlev

    def backward_halo(bar, surf_bar):
        return jnp.concatenate([bar[64:128], div_bar(bar, surf_bar)])

    def adjoint(bar, surf_bar, halos):
        a_u, a_v = bar[:64], bar[64:128]
        hb = dx(a_u) + halos[:64]
        change = jnp.concatenate(
            [-dx(div_bar(bar, surf_bar)) - sin_lat * a_v, -halos[64:] + sin_lat * a_u, weight * rising(hb)]
        )
        return change, jnp.sum(hb, 0)

    def pick(values):
        return values[sample, row_in_band]

    state0, surf0 = x0.astype(jnp.float32), pick(surface)
    bar0, sbar0 = t0.astype(jnp.float32), TIME_STEP * pick(cot_surface)
    halos = halo(jnp.concatenate([forward_halo(state0, surf0), backward_halo(bar0, sbar0)]))
    tend0, kept0 = mlp(x0)
    dyn, dyn_surf = dynamics(state0, surf0, halos[:128])
    inc_a = TIME_STEP * (dyn + tend0.astype(jnp.float32))
    sinc_a = TIME_STEP * dyn_surf
    state1, surf1 = state0 + inc_a, surf0 + sinc_a
    x1 = state1.astype(jnp.bfloat16)
    halos1 = halo(forward_halo(state1, surf1))
    tend1, kept1 = mlp(x1)
    dyn, dyn_surf = dynamics(state1, surf1, halos1)
    inc = inc_a + TIME_STEP * (dyn + tend1.astype(jnp.float32))
    sinc = sinc_a + TIME_STEP * dyn_surf
    adj, adj_surf = adjoint(bar0, sbar0, halos[128:])
    input_bar, grads1 = mlp_back(x1, t0, kept1)
    ginc_a, gsinc_a = adj + input_bar, adj_surf
    bar1, sbar1 = bar0 + TIME_STEP * ginc_a, sbar0 + TIME_STEP * gsinc_a
    halos1 = halo(backward_halo(bar1, sbar1))
    input_bar, grads0 = mlp_back(x0, bar1.astype(jnp.bfloat16), kept0)
    adj, adj_surf = adjoint(bar1, sbar1, halos1)
    ginc, gsinc = ginc_a + adj + input_bar, gsinc_a + adj_surf

    def outgoing(change, surf_change):
        high = surf_change.astype(jnp.bfloat16)
        low = (surf_change - high.astype(jnp.float32)).astype(jnp.bfloat16)
        levels = change.astype(jnp.bfloat16).reshape(3, 8, 8, 360).transpose(1, 0, 2, 3).reshape(8, 24, 360)
        flat = jnp.broadcast_to(jnp.stack([high, low])[None], (8, 2, 360))
        return jnp.concatenate([levels, flat], axis=1)

    def returned(values):
        came = lax.all_to_all(values, GROUP, split_axis=0, concat_axis=0, tiled=True).astype(jnp.float32)
        levels = came[:, :24].reshape(2, 2, 2, 3, 8, 360).transpose(3, 4, 0, 2, 1, 5).reshape(3, 8, 4, 2, 360)
        flat = (came[:, 24] + came[:, 25]).reshape(2, 2, 2, 360).transpose(0, 2, 1, 3).reshape(4, 2, 360)
        return levels, flat

    df, ds = returned(outgoing(inc, sinc))
    dg, dgs = returned(outgoing(ginc, gsinc))

    total = jax.tree.map(jnp.add, grads0, grads1)
    shapes = [g.shape for g in total]
    packed = jnp.concatenate([g.reshape(-1) for g in total])
    count = packed.shape[0]
    packed = jnp.pad(packed, (0, 512 * 640 - count)).astype(jnp.bfloat16)

    def swap(values, axes):
        return lax.all_to_all(values, axes, split_axis=0, concat_axis=0, tiled=True)

    part = swap(packed.reshape(tiles, -1), "tile").astype(jnp.float32).sum(0).astype(jnp.bfloat16)
    part = swap(part.reshape(8, -1), GROUP).astype(jnp.float32).sum(0).astype(jnp.bfloat16)
    part = swap(jnp.broadcast_to(part[None], (8, part.shape[0])), GROUP).reshape(-1)
    full = swap(jnp.broadcast_to(part[None], (tiles, part.shape[0])), "tile").reshape(-1).astype(jnp.float32)
    outs, at = [], 0
    for s in shapes:
        size = s[0] * s[1]
        outs.append(full[at : at + size].reshape(s))
        at += size
    return (fields + df, surface + ds, cot_fields + dg, cot_surface + dgs, *outs)


def solution(mesh):
    levels = P(None, ("lev", "sec"), None, "tile", None)
    flat = P(None, "tile", None)
    return jax.shard_map(
        on_device,
        mesh=mesh,
        in_specs=(levels, flat, levels, flat, P("tile", None), P(), P(), P(), P()),
        out_specs=(levels, flat, levels, flat, P(), P(), P(), P()),
        check_vma=False,
    )
```

```python
import functools
import math

import jax
import jax.numpy as jnp
from jax import lax
from jax.experimental import pallas as pl
from jax.experimental.pallas import tpu as pltpu
from jax.sharding import PartitionSpec as P

TIME_STEP = 0.1
COS_FLOOR = 0.2
INV_SQRT_TWO = 1.0 / math.sqrt(2.0)
INV_SQRT_TWO_PI = 1.0 / math.sqrt(2.0 * math.pi)
EVERY = ("lev", "tile", "sec")
HIGH = lax.Precision.HIGHEST
MESH = pl.DeviceIdType.MESH
BF = jnp.bfloat16
F32 = jnp.float32
NLEV, NLON, LANES = 64, 360, 384
TILES, GROUP, PLANE, LINE = 64, 8, 32, 16
GROWS = 784
SHARE = 80


def dot(a, b):
    return jnp.dot(a, b, preferred_element_type=F32)


def dot_first(a, b):
    return lax.dot_general(a, b, (((0,), (0,)), ((), ())), preferred_element_type=F32)


def dot_last(a, b):
    return lax.dot_general(a, b, (((1,), (1,)), ((), ())), preferred_element_type=F32)


def kernel(
    sent_a, sent_b, flat, masks, bias, w_in, w_mid, w_out,
    out_f, out_g, g_in, g_mid, g_out,
    ra, rb, hs, hr, st, br, xs, a1, a2, s1, s2, inc, ginc, surf_ref,
    f_s, f_r, b_s, b_r, gacc, gs, gr, zs, zr, za, s80, ag,
    sems, hsem,
):
    lev, tile, sec = (lax.axis_index(a) for a in EVERY)
    r = lax.rem(lev, 2)
    me_g = lev * 2 + sec
    spot = lax.rem(tile, 8)
    z_lo = lax.div(tile, 8)
    me_p = lev * 8 + spot
    me_z = sec * 8 + z_lo

    def of_group(q):
        return (lax.div(q, 2), tile, lax.rem(q, 2))

    def of_plane(q):
        return (lax.div(q, 8), z_lo * 8 + lax.rem(q, 8), sec)

    def of_line(q):
        return (lev, lax.rem(q, 8) * 8 + spot, lax.div(q, 8))

    above = (lev + 1 - 2 * r, lax.rem(tile + r, TILES), sec)
    below_dev = (lev + 1 - 2 * r, lax.rem(tile + TILES - 1 + r, TILES), sec)

    barrier = pltpu.get_barrier_semaphore()

    def greet(where):
        pl.semaphore_signal(barrier, inc=1, device_id=where, device_id_type=MESH)

    def each(n, me, act):
        def go(p, c):
            act(lax.rem(me + p, n))
            return c

        lax.fori_loop(1, n, go, 0)

    each(GROUP, me_g, lambda q: greet(of_group(q)))
    greet(above)
    greet(below_dev)
    each(PLANE, me_p, lambda q: greet(of_plane(q)))
    each(LINE, me_z, lambda q: greet(of_line(q)))
    pl.semaphore_wait(barrier, GROUP - 1 + 2 + PLANE - 1 + LINE - 1)

    def push(src, dst, k, where):
        pltpu.make_async_remote_copy(
            src_ref=src, dst_ref=dst, send_sem=sems.at[2 * k], recv_sem=sems.at[2 * k + 1],
            device_id=where, device_id_type=MESH,
        ).start()

    def finish(ref, sem):
        pltpu.make_async_copy(ref, ref, sem).wait()

    each(GROUP, me_g, lambda q: push(sent_a.at[q], ra.at[me_g], 0, of_group(q)))
    each(GROUP, me_g, lambda q: push(sent_b.at[q], rb.at[me_g], 1, of_group(q)))

    lane = lax.broadcasted_iota(jnp.int32, (64, LANES), 1)
    real = lane < NLON
    level = lax.broadcasted_iota(jnp.int32, (64, LANES), 0).astype(F32)
    weight = 1.0 / (level + 1.0)
    row_i = lax.broadcasted_iota(jnp.int32, (64, 64), 0)
    col_i = lax.broadcasted_iota(jnp.int32, (64, 64), 1)
    tri_rise = jnp.where(row_i >= col_i, 1.0, 0.0).astype(F32)
    tri_fall = jnp.where(row_i <= col_i, 1.0, 0.0).astype(F32)
    x_factor, sin_lat = flat[3:4, :], flat[4:5, :]
    has_before, has_after = flat[5:6, :] > 0, flat[6:7, :] > 0
    land = flat[2:3, :] > 0

    def rising(values):
        return jnp.dot(tri_rise, values, precision=HIGH, preferred_element_type=F32)

    def falling(values):
        return jnp.dot(tri_fall, values, precision=HIGH, preferred_element_type=F32)

    def dx(values):
        rows = values.shape[0]
        ln = lax.broadcasted_iota(jnp.int32, (rows, LANES), 1)
        full = jnp.where(ln == NLON, pltpu.roll(values, NLON, 1), values)
        full = jnp.where(ln == LANES - 1, pltpu.roll(values, LANES - NLON, 1), full)
        return (pltpu.roll(full, LANES - 1, 1) - pltpu.roll(full, 1, 1)) * x_factor

    def halo_send(k, first, second):
        hs[k, 0:64, :] = first.astype(BF)
        hs[k, 64:128, :] = second.astype(BF)
        for way, where in ((0, above), (1, below_dev)):
            pltpu.make_async_remote_copy(
                src_ref=hs.at[k], dst_ref=hr.at[k, way], send_sem=hsem.at[k, way, 0],
                recv_sem=hsem.at[k, way, 1], device_id=where, device_id_type=MESH,
            ).start()

    def halo_take(k):
        for way in (0, 1):
            finish(hr.at[k, way], hsem.at[k, way, 1])
        before, after = hr[k, 0].astype(F32), hr[k, 1].astype(F32)
        zero = jnp.zeros((), F32)
        diff = (jnp.where(has_after, after, zero) - jnp.where(has_before, before, zero)) * 0.5
        return diff[0:64], diff[64:128]

    def forward(k):
        pre = dot_first(w_in[...], xs[k, 0:192, :]) + jnp.where(land, bias[:, 1:2], bias[:, 0:1])
        keep(pre, a1, s1, k)
        keep(dot_first(w_mid[...], a1[k]), a2, s2, k)
        return dot_first(w_out[...], a2[k]).astype(BF).astype(F32)

    def keep(pre, act, slope, k):
        cumulative = 0.5 * (1.0 + lax.erf(pre * INV_SQRT_TWO))
        density = jnp.exp(-0.5 * pre * pre) * INV_SQRT_TWO_PI
        act[k] = (pre * cumulative).astype(BF)
        slope[k] = cumulative + pre * density

    def backward(k, tend_bar):
        second_bar = (dot(w_out[...], tend_bar) * s2[k]).astype(BF)
        first_bar = (dot(w_mid[...], second_bar) * s1[k]).astype(BF)
        return second_bar, first_bar, dot(w_in[...], first_bar).astype(BF).astype(F32)

    def gradients(k, tend_bar, second_bar, first_bar):
        return (
            (0, dot_last(xs[k], first_bar)),
            (208, dot_last(a1[k], second_bar)),
            (592, dot_last(tend_bar, a2[k])),
        )

    def dynamics(surf, dv, dh):
        u, v, t = st[0:64, :], st[64:128, :], st[128:192, :]
        div = dx(u) + dv
        height = falling(weight * t) + surf
        flux = rising(div) * (1.0 / NLEV)
        return (
            -dx(height) + sin_lat * v, -dh - sin_lat * u, -flux,
            jnp.sum(div, axis=0, keepdims=True) * (-1.0 / NLEV),
        )

    def div_bar(surf_bar):
        return (-falling(br[128:192, :]) - surf_bar) * (1.0 / NLEV)

    def adjoint(surf_bar, da, ddb):
        a_u, a_v = br[0:64, :], br[64:128, :]
        hb = dx(a_u) + da
        return (
            -dx(div_bar(surf_bar)) - sin_lat * a_v, -ddb + sin_lat * a_u, weight * rising(hb),
            jnp.sum(hb, axis=0, keepdims=True),
        )

    def give(src, change, surf_change, dst, k):
        high = surf_change.astype(BF)
        low = (surf_change - high.astype(F32)).astype(BF)
        rows = lax.broadcasted_iota(jnp.int32, (8, LANES), 0)
        tail = jnp.where(rows == 0, high.astype(F32), jnp.where(rows == 1, low.astype(F32), 0.0))
        for g in range(GROUP):
            parts = [change[f * 64 + g * 8 : f * 64 + g * 8 + 8, :] for f in range(3)]
            src[g] = jnp.concatenate(parts + [tail], axis=0).astype(BF)
        dst[me_g] = src[me_g]
        each(GROUP, me_g, lambda q: push(src.at[q], dst.at[me_g], k, of_group(q)))

    xs[0, 192:208, :] = masks[...]
    xs[1, 192:208, :] = masks[...]
    ra[me_g] = sent_a[me_g]
    rb[me_g] = sent_b[me_g]
    surf0, sbar0 = flat[0:1, :], flat[1:2, :]

    finish(ra.at[pl.ds(0, 7)], sems.at[1])
    for g in range(GROUP):
        a = ra[g].astype(F32)
        for f in range(3):
            st[f * 64 + g * 8 : f * 64 + g * 8 + 8, :] = a[f * 8 : f * 8 + 8]
        br[g * 8 : g * 8 + 8, :] = a[24:32]
    halo_send(0, st[64:128, :], falling(weight * st[128:192, :]) + surf0)
    xs[0, 0:192, :] = st[...].astype(BF)
    tend = forward(0)

    finish(rb.at[pl.ds(0, 7)], sems.at[3])
    for g in range(GROUP):
        b = rb[g].astype(F32)
        br[64 + g * 8 : 72 + g * 8, :] = b[0:8]
        br[128 + g * 8 : 136 + g * 8, :] = b[8:16]
    halo_send(1, br[64:128, :], div_bar(sbar0))

    du, dv, dt, dsurf = dynamics(surf0, *halo_take(0))
    for i, d in enumerate((du, dv, dt)):
        at = slice(64 * i, 64 * i + 64)
        change = TIME_STEP * (d + tend[at])
        inc[at, :] = change
        st[at, :] = st[at, :] + change
    surf_inc = TIME_STEP * dsurf
    surf1 = surf0 + surf_inc
    halo_send(2, st[64:128, :], falling(weight * st[128:192, :]) + surf1)
    xs[1, 0:192, :] = st[...].astype(BF)
    tend = forward(1)

    t0 = br[...].astype(BF)
    second_bar, first_bar, input_bar = backward(1, t0)
    au, av, at_, asurf = adjoint(sbar0, *halo_take(1))
    for i, d in enumerate((au, av, at_)):
        at = slice(64 * i, 64 * i + 64)
        change = d + input_bar[at]
        ginc[at, :] = change
        br[at, :] = jnp.where(real, br[at, :] + TIME_STEP * change, 0.0)
    gsurf = asurf
    sbar1 = sbar0 + TIME_STEP * asurf
    halo_send(3, br[64:128, :], div_bar(sbar1))

    du, dv, dt, dsurf = dynamics(surf1, *halo_take(2))
    for i, d in enumerate((du, dv, dt)):
        at = slice(64 * i, 64 * i + 64)
        inc[at, :] = inc[at, :] + TIME_STEP * (d + tend[at])
    give(f_s, inc, surf_inc + TIME_STEP * dsurf, f_r, 2)

    for at, g in gradients(1, t0, second_bar, first_bar):
        gacc[at : at + g.shape[0], :] = g

    t1 = br[...].astype(BF)
    second_bar, first_bar, input_bar = backward(0, t1)
    gs[3 * GROWS :, :] = jnp.zeros((PLANE * SHARE - 3 * GROWS, 128), BF)
    for at, g in gradients(0, t1, second_bar, first_bar):
        total = (gacc[at : at + g.shape[0], :] + g).astype(BF)
        for b in range(3):
            gs[GROWS * b + at : GROWS * b + at + g.shape[0], :] = total[:, 128 * b : 128 * b + 128]

    def share(ref, q):
        return ref.at[pl.ds(pl.multiple_of(q * SHARE, 16), SHARE)]

    each(PLANE, me_p, lambda q: push(share(gs, q), gr.at[me_p], 3, of_plane(q)))

    au, av, at_, asurf = adjoint(sbar1, *halo_take(3))
    for i, d in enumerate((au, av, at_)):
        at = slice(64 * i, 64 * i + 64)
        ginc[at, :] = ginc[at, :] + d + input_bar[at]
    give(b_s, ginc, gsurf + asurf, b_r, 4)

    finish(gr.at[pl.ds(0, PLANE - 1)], sems.at[7])
    mine = gs[pl.ds(pl.multiple_of(me_p * SHARE, 16), SHARE), :].astype(F32)
    s80[...] = lax.fori_loop(
        1, PLANE, lambda p, acc: acc + gr[lax.rem(me_p + p, PLANE)].astype(F32), mine
    )
    for k in range(LINE):
        zs[k, 0:5, :] = s80[5 * k : 5 * k + 5, :]
        zs[k, 5:8, :] = jnp.zeros((3, 128), F32)
    each(LINE, me_z, lambda q: push(zs.at[q], zr.at[me_z], 5, of_line(q)))
    finish(zr.at[pl.ds(0, LINE - 1)], sems.at[11])
    za[me_z] = lax.fori_loop(
        1, LINE, lambda p, acc: acc + zr[lax.rem(me_z + p, LINE)], zs[me_z]
    )
    each(LINE, me_z, lambda q: push(za.at[me_z], za.at[me_z], 6, of_line(q)))
    finish(za.at[pl.ds(0, LINE - 1)], sems.at[13])
    for k in range(LINE):
        s80[5 * k : 5 * k + 5, :] = za[k, 0:5, :]
    ag[pl.ds(pl.multiple_of(me_p * SHARE, 16), SHARE), :] = s80[...].astype(BF)
    each(PLANE, me_p, lambda q: push(share(ag, me_p), share(ag, me_p), 7, of_plane(q)))

    finish(f_r.at[pl.ds(0, 7)], sems.at[5])
    out_f[...] = f_r[...]
    finish(b_r.at[pl.ds(0, 7)], sems.at[9])
    out_g[...] = b_r[...]
    finish(ag.at[pl.ds(0, (PLANE - 1) * SHARE)], sems.at[15])
    for b in range(3):
        lanes = slice(128 * b, 128 * b + 128)
        base = GROWS * b
        g_in[:, lanes] = ag[base : base + 208, :].astype(F32)
        g_mid[:, lanes] = ag[base + 208 : base + 592, :].astype(F32)
        g_out[:, lanes] = ag[base + 592 : base + 784, :].astype(F32)

    finish(ra.at[pl.ds(0, 7)], sems.at[0])
    finish(rb.at[pl.ds(0, 7)], sems.at[2])
    finish(f_s.at[pl.ds(0, 7)], sems.at[4])
    finish(gr.at[pl.ds(0, PLANE - 1)], sems.at[6])
    finish(b_s.at[pl.ds(0, 7)], sems.at[8])
    finish(zs.at[pl.ds(0, LINE - 1)], sems.at[10])
    finish(zs.at[pl.ds(0, LINE - 1)], sems.at[12])
    finish(ag.at[pl.ds(0, (PLANE - 1) * SHARE)], sems.at[14])
    for k in range(4):
        for way in (0, 1):
            finish(hs.at[k], hsem.at[k, way, 0])


def call(*operands):
    def v(shape, dtype):
        return pltpu.VMEM(shape, dtype)

    slab = (GROUP, 32, LANES)
    hidden = (2, 384, LANES)
    return pl.pallas_call(
        kernel,
        out_shape=(
            jax.ShapeDtypeStruct(slab, BF),
            jax.ShapeDtypeStruct(slab, BF),
            jax.ShapeDtypeStruct((208, 384), F32),
            jax.ShapeDtypeStruct((384, 384), F32),
            jax.ShapeDtypeStruct((192, 384), F32),
        ),
        in_specs=[pl.BlockSpec(memory_space=pltpu.VMEM)] * 8,
        out_specs=tuple([pl.BlockSpec(memory_space=pltpu.VMEM)] * 5),
        scratch_shapes=[
            v(slab, BF), v((GROUP, 16, LANES), BF),
            v((4, 128, LANES), BF), v((4, 2, 128, LANES), BF),
            v((192, LANES), F32), v((192, LANES), F32), v((2, 208, LANES), BF),
            v(hidden, BF), v(hidden, BF), v(hidden, F32), v(hidden, F32),
            v((192, LANES), F32), v((192, LANES), F32), v((8, LANES), F32),
            v(slab, BF), v(slab, BF), v(slab, BF), v(slab, BF),
            v((GROWS, 384), F32), v((PLANE * SHARE, 128), BF), v((PLANE, SHARE, 128), BF),
            v((LINE, 8, 128), F32), v((LINE, 8, 128), F32), v((LINE, 8, 128), F32),
            v((SHARE, 128), F32), v((PLANE * SHARE, 128), BF),
            pltpu.SemaphoreType.DMA((16,)), pltpu.SemaphoreType.DMA((4, 2, 2)),
        ],
        compiler_params=pltpu.CompilerParams(
            collective_id=0, has_side_effects=True, vmem_limit_bytes=40 * 2**20
        ),
        name="window",
    )(*operands)


def on_device(fields, surface, cot_fields, cot_surface, land_sea, w_in, w_mid, w_out, bias_in):
    lev_i, tile_i, sec_i = (lax.axis_index(a) for a in EVERY)
    row_in_band = lax.rem(lev_i, 2)
    sample = lax.div(lev_i, 2) * 2 + sec_i
    row = tile_i * 2 + row_in_band
    latitude = -0.5 * math.pi + (row.astype(F32) + 0.5) * (math.pi / (2 * TILES))
    x_factor = 0.5 / jnp.maximum(jnp.cos(latitude), COS_FLOOR)
    sin_lat = jnp.sin(latitude)

    def pad(values):
        return jnp.pad(values, [(0, 0)] * (values.ndim - 1) + [(0, LANES - NLON)])

    def to_columns(values):
        split = values.astype(BF).reshape(3, 8, 2, 2, 2, NLON)
        return pad(split.transpose(2, 4, 3, 0, 1, 5).reshape(8, 24, NLON))

    sent = jnp.concatenate([to_columns(fields), to_columns(TIME_STEP * cot_fields)], axis=1)
    mask = land_sea[row_in_band] > 0

    def line(value):
        return jnp.broadcast_to(value, (NLON,)).astype(F32)

    flat = pad(
        jnp.stack(
            [
                surface[sample, row_in_band],
                TIME_STEP * cot_surface[sample, row_in_band],
                mask.astype(F32),
            ]
        )
    )
    consts = jnp.stack([x_factor, sin_lat, (row > 0).astype(F32), (row < 2 * TILES - 1).astype(F32), 0.0 * x_factor])
    flat = jnp.concatenate([flat, jnp.broadcast_to(consts[:, None], (5, LANES))])
    masks = jnp.pad(jnp.stack([~mask, mask]).astype(BF), ((0, 14), (0, LANES - NLON)))
    came_f, came_g, g_in, g_mid, g_out = call(
        sent[:, :32], sent[:, 32:], flat, masks, bias_in.T, w_in, w_mid, w_out
    )

    def returned(came):
        came = came[:, :, :NLON].astype(F32)
        levels = came[:, :24].reshape(2, 2, 2, 3, 8, NLON).transpose(3, 4, 0, 2, 1, 5).reshape(3, 8, 4, 2, NLON)
        level_flat = (came[:, 24] + came[:, 25]).reshape(2, 2, 2, NLON).transpose(0, 2, 1, 3).reshape(4, 2, NLON)
        return levels, level_flat

    df, ds = returned(came_f)
    dg, dgs = returned(came_g)
    return (
        fields + df,
        surface + ds,
        cot_fields + dg,
        cot_surface + dgs,
        g_in[:192],
        g_mid,
        g_out.T,
        g_in[192:194],
    )


def solution(mesh):
    levels = P(None, ("lev", "sec"), None, "tile", None)
    flat = P(None, "tile", None)
    return jax.shard_map(
        on_device,
        mesh=mesh,
        in_specs=(levels, flat, levels, flat, P("tile", None), P(), P(), P(), P()),
        out_specs=(levels, flat, levels, flat, P(), P(), P(), P()),
        check_vma=False,
    )
```

```python
import functools
import math

import jax
import jax.numpy as jnp
from jax import lax
from jax.experimental import pallas as pl
from jax.experimental.pallas import tpu as pltpu
from jax.sharding import PartitionSpec as P

TIME_STEP = 0.1
COS_FLOOR = 0.2
INV_SQRT_TWO = 1.0 / math.sqrt(2.0)
INV_SQRT_TWO_PI = 1.0 / math.sqrt(2.0 * math.pi)
EVERY = ("lev", "tile", "sec")
HIGH = lax.Precision.HIGHEST
MESH = pl.DeviceIdType.MESH
BF = jnp.bfloat16
F32 = jnp.float32
NLEV, NLON, LANES = 64, 360, 384
TILES, GROUP, PLANE = 64, 8, 32
GROWS = 784
PART = (512, 272)
SHARE = (48, 32)
SLAB = (16, 640)


def dot(a, b):
    return jnp.dot(a, b, preferred_element_type=F32)


def dot_last(a, b):
    return lax.dot_general(a, b, (((1,), (1,)), ((), ())), preferred_element_type=F32)


def kernel(
    sent, consts, surface, cot_surface, land_sea, bias, w_in_h, w_mid_h, w_out_h,
    out_f, out_g, g_in, g_mid, g_out, g_bias,
    w_in, w_mid, w_out, w_in_t, w_mid_t, w_out_t, sv, cv, mv, bv, flat, bmat,
    a_s, b_s, ra, rb, hs, hr, st, br, xs, a1, a2, s1, s2, inc, ginc,
    f_s, f_r, o_s, o_r, gacc, gs0, gs1, gr0, gr1, near0, near1, far0, far1, ag0, ag1,
    sems, hsem, wsem,
):
    lev, tile, sec = (lax.axis_index(a) for a in EVERY)
    r = lax.rem(lev, 2)
    me_g = lev * 2 + sec
    spot = lax.rem(tile, 8)
    z_lo = lax.div(tile, 8)
    me_p = lev * 8 + spot
    pos = lax.rem(z_lo, 4)
    quad = lax.div(z_lo, 4)
    me_f = sec * 2 + quad
    sample = lax.div(lev, 2) * 2 + sec
    gs, gr, near, far, ag = (gs0, gs1), (gr0, gr1), (near0, near1), (far0, far1), (ag0, ag1)

    def of_group(q):
        return (lax.div(q, 2), tile, lax.rem(q, 2))

    def of_plane(q):
        return (lax.div(q, 8), z_lo * 8 + lax.rem(q, 8), sec)

    def of_near(q):
        return (lev, (quad * 4 + q) * 8 + spot, sec)

    def of_far(q):
        return (lev, (lax.rem(q, 2) * 4 + pos) * 8 + spot, lax.div(q, 2))

    above = (lev + 1 - 2 * r, lax.rem(tile + r, TILES), sec)
    below_dev = (lev + 1 - 2 * r, lax.rem(tile + TILES - 1 + r, TILES), sec)

    fetches = [
        pltpu.make_async_copy(src, dst, wsem.at[i])
        for i, (src, dst) in enumerate(
            (
                (surface.at[sample], sv), (cot_surface.at[sample], cv), (land_sea, mv), (bias, bv),
                (w_in_h, w_in), (w_mid_h, w_mid), (w_out_h, w_out_t),
            )
        )
    ]
    for copy in fetches:
        copy.start()

    barrier = pltpu.get_barrier_semaphore()

    def greet(where):
        pl.semaphore_signal(barrier, inc=1, device_id=where, device_id_type=MESH)

    def each(n, me, act):
        def go(p, c):
            act(lax.rem(me + p, n))
            return c

        lax.fori_loop(1, n, go, 0)

    each(GROUP, me_g, lambda q: greet(of_group(q)))
    greet(above)
    greet(below_dev)
    each(PLANE, me_p, lambda q: greet(of_plane(q)))
    each(4, pos, lambda q: greet(of_near(q)))
    each(4, me_f, lambda q: greet(of_far(q)))

    def pack(dst, g, uv, t, rest):
        dst[g, :, 0:384] = uv.astype(BF)
        dst[g, :, 384:512] = jnp.concatenate([t[:, 0:128], t[:, 256:384]], axis=0).astype(BF)
        dst[g, :, 512:640] = jnp.concatenate([t[:, 128:256], rest], axis=0).astype(BF)

    def unpack(slab):
        uv, one, two = slab[:, 0:384], slab[:, 384:512], slab[:, 512:640]
        t = jnp.concatenate([one[0:8], two[0:8], one[8:16]], axis=1)
        return uv[0:8], uv[8:16], t, two[8:16]

    nothing = jnp.zeros((8, 128), F32)
    for g in range(GROUP):
        for base, dst in ((0, a_s), (24, b_s)):
            wide = sent[g, base : base + 24, :].astype(F32)
            pack(dst, g, wide[0:16], wide[16:24], nothing)
    pl.semaphore_wait(barrier, GROUP - 1 + 2 + PLANE - 1 + 3 + 3)

    def push(src, dst, k, where):
        pushed.add(k)
        pltpu.make_async_remote_copy(
            src_ref=src, dst_ref=dst, send_sem=sems.at[2 * k], recv_sem=sems.at[2 * k + 1],
            device_id=where, device_id_type=MESH,
        ).start()

    def finish(ref, sem):
        pltpu.make_async_copy(ref, ref, sem).wait()

    pushed, taken, halos_sent, halos_taken = set(), set(), set(), set()

    def done(ref, i):
        taken.add(i)
        finish(ref, sems.at[i])

    def leave():
        sizes = (
            ra.at[pl.ds(0, 7)], rb.at[pl.ds(0, 7)], f_r.at[pl.ds(0, 7)], o_r.at[pl.ds(0, 7)],
            gr0.at[pl.ds(0, PLANE - 1)], gr1.at[pl.ds(0, PLANE - 1)], near0.at[pl.ds(0, 3)], near1.at[pl.ds(0, 3)],
            far0.at[pl.ds(0, 3)], far1.at[pl.ds(0, 3)],
            ag0.at[pl.ds(0, (PLANE - 1) * SHARE[0])], ag1.at[pl.ds(0, (PLANE - 1) * SHARE[1])],
        )
        for k in sorted(pushed):
            done(sizes[k], 2 * k)
            if 2 * k + 1 not in taken:
                done(sizes[k], 2 * k + 1)
        for k in sorted(halos_sent):
            for way in (0, 1):
                finish(hs.at[k], hsem.at[k, way, 0])
                if k not in halos_taken:
                    finish(hr.at[k, way], hsem.at[k, way, 1])

    each(GROUP, me_g, lambda q: push(a_s.at[q], ra.at[me_g], 0, of_group(q)))
    each(GROUP, me_g, lambda q: push(b_s.at[q], rb.at[me_g], 1, of_group(q)))

    lane = lax.broadcasted_iota(jnp.int32, (64, LANES), 1)
    real = lane < NLON
    level = lax.broadcasted_iota(jnp.int32, (64, LANES), 0).astype(F32)
    weight = 1.0 / (level + 1.0)
    row_i = lax.broadcasted_iota(jnp.int32, (64, 64), 0)
    col_i = lax.broadcasted_iota(jnp.int32, (64, 64), 1)
    tri_rise = jnp.where(row_i >= col_i, 1.0, 0.0).astype(F32)
    tri_fall = jnp.where(row_i <= col_i, 1.0, 0.0).astype(F32)
    x_factor, sin_lat = consts[0:1, :], consts[1:2, :]
    has_before, has_after = consts[2:3, :] > 0, consts[3:4, :] > 0

    def rising(values):
        return jnp.dot(tri_rise, values, precision=HIGH, preferred_element_type=F32)

    def falling(values):
        return jnp.dot(tri_fall, values, precision=HIGH, preferred_element_type=F32)

    def dx(values):
        rows = values.shape[0]
        ln = lax.broadcasted_iota(jnp.int32, (rows, LANES), 1)
        full = jnp.where(ln == NLON, pltpu.roll(values, NLON, 1), values)
        full = jnp.where(ln == LANES - 1, pltpu.roll(values, LANES - NLON, 1), full)
        return (pltpu.roll(full, LANES - 1, 1) - pltpu.roll(full, 1, 1)) * x_factor

    def halo_send(k, first, second):
        halos_sent.add(k)
        hs[k, 0:64, :] = first.astype(BF)
        hs[k, 64:128, :] = second.astype(BF)
        for way, where in ((0, above), (1, below_dev)):
            pltpu.make_async_remote_copy(
                src_ref=hs.at[k], dst_ref=hr.at[k, way], send_sem=hsem.at[k, way, 0],
                recv_sem=hsem.at[k, way, 1], device_id=where, device_id_type=MESH,
            ).start()

    def halo_take(k):
        halos_taken.add(k)
        for way in (0, 1):
            finish(hr.at[k, way], hsem.at[k, way, 1])
        before, after = hr[k, 0].astype(F32), hr[k, 1].astype(F32)
        zero = jnp.zeros((), F32)
        diff = (jnp.where(has_after, after, zero) - jnp.where(has_before, before, zero)) * 0.5
        return diff[0:64], diff[64:128]

    def forward(k):
        pre = dot(w_in_t[...], xs[k, 0:192, :]) + bmat[...]
        keep(pre, a1, s1, k)
        keep(dot(w_mid_t[...], a1[k]), a2, s2, k)
        return dot(w_out_t[...], a2[k]).astype(BF).astype(F32)

    def keep(pre, act, slope, k):
        cumulative = 0.5 * (1.0 + lax.erf(pre * INV_SQRT_TWO))
        density = jnp.exp(-0.5 * pre * pre) * INV_SQRT_TWO_PI
        act[k] = (pre * cumulative).astype(BF)
        slope[k] = cumulative + pre * density

    def backward(k, tend_bar):
        second_bar = (dot(w_out[...], tend_bar) * s2[k]).astype(BF)
        first_bar = (dot(w_mid[...], second_bar) * s1[k]).astype(BF)
        return second_bar, first_bar, dot(w_in[...], first_bar).astype(BF).astype(F32)

    def gradients(k, tend_bar, second_bar, first_bar):
        return (
            (0, dot_last(tend_bar, a2[k])),
            (192, dot_last(a1[k], second_bar)),
            (576, dot_last(xs[k], first_bar)),
        )

    def dynamics(surf, dv, dh):
        u, v, t = st[0:64, :], st[64:128, :], st[128:192, :]
        div = dx(u) + dv
        height = falling(weight * t) + surf
        flux = rising(div) * (1.0 / NLEV)
        return (
            -dx(height) + sin_lat * v, -dh - sin_lat * u, -flux,
            jnp.sum(div, axis=0, keepdims=True) * (-1.0 / NLEV),
        )

    def div_bar(surf_bar):
        return (-falling(br[128:192, :]) - surf_bar) * (1.0 / NLEV)

    def adjoint(surf_bar, da, ddb):
        a_u, a_v = br[0:64, :], br[64:128, :]
        hb = dx(a_u) + da
        return (
            -dx(div_bar(surf_bar)) - sin_lat * a_v, -ddb + sin_lat * a_u, weight * rising(hb),
            jnp.sum(hb, axis=0, keepdims=True),
        )

    def give(src, change, surf_change, dst, k):
        high = surf_change.astype(BF)
        low = (surf_change - high.astype(F32)).astype(BF)
        rows = lax.broadcasted_iota(jnp.int32, (8, 128), 0)
        tail = nothing
        for i in range(6):
            block = (high, low)[i // 3].astype(F32)[:, 128 * (i % 3) : 128 * (i % 3) + 128]
            tail = jnp.where(rows == i, block, tail)
        for g in range(GROUP):
            u, v, t = (change[f * 64 + g * 8 : f * 64 + g * 8 + 8, :] for f in range(3))
            pack(src, g, jnp.concatenate([u, v], axis=0), t, tail)
        dst[me_g] = src[me_g]
        each(GROUP, me_g, lambda q: push(src.at[q], dst.at[me_g], k, of_group(q)))

    ra[me_g] = a_s[me_g]
    rb[me_g] = b_s[me_g]
    for copy in fetches:
        copy.wait()
    flat[...] = jnp.zeros_like(flat)
    flat[0:1, 0:NLON] = jnp.where(r == 0, sv[0:1, :], sv[1:2, :])
    flat[1:2, 0:NLON] = TIME_STEP * jnp.where(r == 0, cv[0:1, :], cv[1:2, :])
    flat[2:3, 0:NLON] = jnp.where(jnp.where(r == 0, mv[0:1, :], mv[1:2, :]) > 0, 1.0, 0.0)
    land = flat[2:3, :] > 0
    mask_row = lax.broadcasted_iota(jnp.int32, (16, LANES), 0)
    sea_or_land = jnp.where(land, 1, 0)
    hot = jnp.where((mask_row == sea_or_land) & (lax.broadcasted_iota(jnp.int32, (16, LANES), 1) < NLON), 1.0, 0.0)
    xs[0, 192:208, :] = hot.astype(BF)
    xs[1, 192:208, :] = hot.astype(BF)
    bias_row = lax.broadcasted_iota(jnp.int32, (8, 384), 0)
    both = jnp.where(bias_row == 0, bv[0:1, :], jnp.where(bias_row == 1, bv[1:2, :], 0.0))
    bmat[...] = lax.dot_general(both, hot[0:8], (((0,), (0,)), ((), ())), precision=HIGH, preferred_element_type=F32)
    w_in_t[...] = w_in[...].T
    w_mid_t[...] = w_mid[...].T
    w_out[...] = w_out_t[...].T
    surf0, sbar0 = flat[0:1, :], flat[1:2, :]

    done(ra.at[pl.ds(0, 7)], 1)
    for g in range(GROUP):
        u, v, t, _ = unpack(ra[g].astype(F32))
        for f, part in enumerate((u, v, t)):
            st[f * 64 + g * 8 : f * 64 + g * 8 + 8, :] = part
    halo_send(0, st[64:128, :], falling(weight * st[128:192, :]) + surf0)
    xs[0, 0:192, :] = st[...].astype(BF)
    tend = forward(0)

    done(rb.at[pl.ds(0, 7)], 3)
    for g in range(GROUP):
        u, v, t, _ = unpack(rb[g].astype(F32))
        for f, part in enumerate((u, v, t)):
            br[f * 64 + g * 8 : f * 64 + g * 8 + 8, :] = part
    halo_send(1, br[64:128, :], div_bar(sbar0))

    du, dv, dt, dsurf = dynamics(surf0, *halo_take(0))
    for i, d in enumerate((du, dv, dt)):
        at = slice(64 * i, 64 * i + 64)
        change = TIME_STEP * (d + tend[at])
        inc[at, :] = change
        st[at, :] = st[at, :] + change
    surf_inc = TIME_STEP * dsurf
    surf1 = surf0 + surf_inc
    halo_send(2, st[64:128, :], falling(weight * st[128:192, :]) + surf1)
    xs[1, 0:192, :] = st[...].astype(BF)
    tend = forward(1)

    t0 = br[...].astype(BF)
    second_bar, first_bar, input_bar = backward(1, t0)
    au, av, at_, asurf = adjoint(sbar0, *halo_take(1))
    for i, d in enumerate((au, av, at_)):
        at = slice(64 * i, 64 * i + 64)
        change = d + input_bar[at]
        ginc[at, :] = change
        br[at, :] = jnp.where(real, br[at, :] + TIME_STEP * change, 0.0)
    gsurf = asurf
    sbar1 = sbar0 + TIME_STEP * asurf
    halo_send(3, br[64:128, :], div_bar(sbar1))

    du, dv, dt, dsurf = dynamics(surf1, *halo_take(2))
    for i, d in enumerate((du, dv, dt)):
        at = slice(64 * i, 64 * i + 64)
        inc[at, :] = inc[at, :] + TIME_STEP * (d + tend[at])
    give(f_s, inc, surf_inc + TIME_STEP * dsurf, f_r, 2)

    for at, g in gradients(1, t0, second_bar, first_bar):
        gacc[at : at + g.shape[0], :] = g

    def share(ref, q, part):
        return ref.at[pl.ds(pl.multiple_of(q * SHARE[part], 16), SHARE[part])]

    def stage(total, at, part):
        for b in range(3):
            base = PART[part] * b + at
            gs[part][base : base + total.shape[0], :] = total[:, 128 * b : 128 * b + 128].astype(BF)

    def scatter(part):
        each(PLANE, me_p, lambda q: push(share(gs[part], q, part), gr[part].at[me_p], 4 + part, of_plane(q)))

    gs1[3 * PART[1] :, :] = jnp.zeros((PLANE * SHARE[1] - 3 * PART[1], 128), BF)
    t1 = br[...].astype(BF)
    second_bar = (dot(w_out[...], t1) * s2[0]).astype(BF)
    stage(gacc[0:192, :] + dot_last(t1, a2[0]), 0, 0)
    mid = gacc[192:576, :] + dot_last(a1[0], second_bar)
    stage(mid[0:320], 192, 0)
    stage(mid[320:384], 0, 1)
    scatter(0)
    first_bar = (dot(w_mid[...], second_bar) * s1[0]).astype(BF)
    stage(gacc[576:784, :] + dot_last(xs[0], first_bar), 64, 1)
    scatter(1)
    input_bar = dot(w_in[...], first_bar).astype(BF).astype(F32)

    au, av, at_, asurf = adjoint(sbar1, *halo_take(3))
    for i, d in enumerate((au, av, at_)):
        at = slice(64 * i, 64 * i + 64)
        ginc[at, :] = ginc[at, :] + d + input_bar[at]
    give(o_s, ginc, gsurf + asurf, o_r, 3)

    def sum_plane(part):
        done(gr[part].at[pl.ds(0, PLANE - 1)], 2 * (4 + part) + 1)
        mine = gs[part][pl.ds(pl.multiple_of(me_p * SHARE[part], 16), SHARE[part]), :].astype(F32)
        near[part][pos] = lax.fori_loop(
            1, PLANE, lambda p, acc: acc + gr[part][lax.rem(me_p + p, PLANE)].astype(F32), mine
        )
        each(4, pos, lambda q: push(near[part].at[pos], near[part].at[pos], 6 + part, of_near(q)))

    def sum_near(part):
        done(near[part].at[pl.ds(0, 3)], 2 * (6 + part) + 1)
        n = near[part]
        far[part][me_f] = ((n[0] + n[1]) + (n[2] + n[3])).astype(BF)
        each(4, me_f, lambda q: push(far[part].at[me_f], far[part].at[me_f], 8 + part, of_far(q)))

    def sum_far(part):
        done(far[part].at[pl.ds(0, 3)], 2 * (8 + part) + 1)
        f = [far[part][i].astype(F32) for i in range(4)]
        at = pl.ds(pl.multiple_of(me_p * SHARE[part], 16), SHARE[part])
        ag[part][at, :] = ((f[0] + f[1]) + (f[2] + f[3])).astype(BF)
        each(PLANE, me_p, lambda q: push(share(ag[part], me_p, part), share(ag[part], me_p, part), 10 + part, of_plane(q)))

    sum_plane(0)
    sum_plane(1)
    sum_near(0)
    sum_near(1)
    sum_far(0)
    sum_far(1)

    def columns_out(came, out):
        for g in range(GROUP):
            u, v, t, rest = unpack(came[g].astype(F32))
            high = jnp.concatenate([rest[0:1], rest[1:2], rest[2:3]], axis=1)
            low = jnp.concatenate([rest[3:4], rest[4:5], rest[5:6]], axis=1)
            row = lax.broadcasted_iota(jnp.int32, (8, LANES), 0)
            tail = jnp.where(row == 0, high, jnp.where(row == 1, low, 0.0))
            out[g] = jnp.concatenate([u, v, t, tail], axis=0).astype(BF)

    done(f_r.at[pl.ds(0, 7)], 5)
    columns_out(f_r, out_f)
    done(o_r.at[pl.ds(0, 7)], 7)
    columns_out(o_r, out_g)

    def taken_from(part, b, first, last):
        base = PART[part] * b
        return ag[part][base + first : base + last, :].astype(F32)

    done(ag0.at[pl.ds(0, (PLANE - 1) * SHARE[0])], 21)
    for b in range(3):
        lanes = slice(128 * b, 128 * b + 128)
        g_out[:, lanes] = taken_from(0, b, 0, 192)
        g_mid[0:320, lanes] = taken_from(0, b, 192, 512)
    done(ag1.at[pl.ds(0, (PLANE - 1) * SHARE[1])], 23)
    for b in range(3):
        lanes = slice(128 * b, 128 * b + 128)
        g_mid[320:384, lanes] = taken_from(1, b, 0, 64)
        g_in[:, lanes] = taken_from(1, b, 64, 256)
        g_bias[:, lanes] = taken_from(1, b, 256, 272)[0:2]
    leave()


def call(*operands):
    def v(shape, dtype):
        return pltpu.VMEM(shape, dtype)

    slab = (GROUP, *SLAB)
    hidden = (2, 384, LANES)
    hbm, vmem = pl.BlockSpec(memory_space=pl.ANY), pl.BlockSpec(memory_space=pltpu.VMEM)
    return pl.pallas_call(
        kernel,
        out_shape=(
            jax.ShapeDtypeStruct((GROUP, 32, LANES), BF),
            jax.ShapeDtypeStruct((GROUP, 32, LANES), BF),
            jax.ShapeDtypeStruct((192, 384), F32),
            jax.ShapeDtypeStruct((384, 384), F32),
            jax.ShapeDtypeStruct((192, 384), F32),
            jax.ShapeDtypeStruct((2, 384), F32),
        ),
        in_specs=[vmem] * 2 + [hbm] * 7,
        out_specs=tuple([vmem] * 6),
        scratch_shapes=[
            v((192, 384), BF), v((384, 384), BF), v((384, 192), BF),
            v((384, 192), BF), v((384, 384), BF), v((192, 384), BF),
            v((2, NLON), F32), v((2, NLON), F32), v((2, NLON), jnp.int32), v((2, 384), F32),
            v((8, LANES), F32), v((384, LANES), F32),
            v(slab, BF), v(slab, BF), v(slab, BF), v(slab, BF),
            v((4, 128, LANES), BF), v((4, 2, 128, LANES), BF),
            v((192, LANES), F32), v((192, LANES), F32), v((2, 208, LANES), BF),
            v(hidden, BF), v(hidden, BF), v(hidden, F32), v(hidden, F32),
            v((192, LANES), F32), v((192, LANES), F32),
            v(slab, BF), v(slab, BF), v(slab, BF), v(slab, BF),
            v((GROWS, 384), F32),
            v((PLANE * SHARE[0], 128), BF), v((PLANE * SHARE[1], 128), BF),
            v((PLANE, SHARE[0], 128), BF), v((PLANE, SHARE[1], 128), BF),
            v((4, SHARE[0], 128), F32), v((4, SHARE[1], 128), F32),
            v((4, SHARE[0], 128), BF), v((4, SHARE[1], 128), BF),
            v((PLANE * SHARE[0], 128), BF), v((PLANE * SHARE[1], 128), BF),
            pltpu.SemaphoreType.DMA((24,)), pltpu.SemaphoreType.DMA((4, 2, 2)), pltpu.SemaphoreType.DMA((7,)),
        ],
        compiler_params=pltpu.CompilerParams(
            collective_id=0, has_side_effects=True, vmem_limit_bytes=40 * 2**20
        ),
        name="window",
    )(*operands)


def on_device(fields, surface, cot_fields, cot_surface, land_sea, w_in, w_mid, w_out, bias_in):
    lev_i, tile_i = lax.axis_index("lev"), lax.axis_index("tile")
    row_in_band = lax.rem(lev_i, 2)
    row = tile_i * 2 + row_in_band
    latitude = -0.5 * math.pi + (row.astype(F32) + 0.5) * (math.pi / (2 * TILES))
    x_factor = 0.5 / jnp.maximum(jnp.cos(latitude), COS_FLOOR)
    sin_lat = jnp.sin(latitude)

    def pad(values):
        return jnp.pad(values, [(0, 0)] * (values.ndim - 1) + [(0, LANES - NLON)])

    def to_columns(values):
        split = values.astype(BF).reshape(3, 8, 2, 2, 2, NLON)
        return pad(split.transpose(2, 4, 3, 0, 1, 5).reshape(8, 24, NLON))

    sent = jnp.concatenate([to_columns(fields), to_columns(TIME_STEP * cot_fields)], axis=1)
    consts = jnp.stack([x_factor, sin_lat, (row > 0).astype(F32), (row < 2 * TILES - 1).astype(F32)])
    consts = jnp.broadcast_to(jnp.concatenate([consts, consts])[:, None], (8, LANES))
    came_f, came_g, g_in, g_mid, g_out, g_bias = call(
        sent, consts, surface, cot_surface, land_sea, bias_in, w_in, w_mid, w_out.T
    )

    def returned(came):
        came = came[:, :, :NLON].astype(F32)
        levels = came[:, :24].reshape(2, 2, 2, 3, 8, NLON).transpose(3, 4, 0, 2, 1, 5).reshape(3, 8, 4, 2, NLON)
        level_flat = (came[:, 24] + came[:, 25]).reshape(2, 2, 2, NLON).transpose(0, 2, 1, 3).reshape(4, 2, NLON)
        return levels, level_flat

    df, ds = returned(came_f)
    dg, dgs = returned(came_g)
    return (
        fields + df,
        surface + ds,
        cot_fields + dg,
        cot_surface + dgs,
        g_in,
        g_mid,
        g_out.T,
        g_bias,
    )


def solution(mesh):
    levels = P(None, ("lev", "sec"), None, "tile", None)
    flat = P(None, "tile", None)
    return jax.shard_map(
        on_device,
        mesh=mesh,
        in_specs=(levels, flat, levels, flat, P("tile", None), P(), P(), P(), P()),
        out_specs=(levels, flat, levels, flat, P(), P(), P(), P()),
        check_vma=False,
    )
```

```python
import functools
import math

import jax
import jax.numpy as jnp
from jax import lax
from jax.experimental import pallas as pl
from jax.experimental.pallas import tpu as pltpu
from jax.sharding import PartitionSpec as P

TIME_STEP = 0.1
COS_FLOOR = 0.2
INV_SQRT_TWO = 1.0 / math.sqrt(2.0)
INV_SQRT_TWO_PI = 1.0 / math.sqrt(2.0 * math.pi)
EVERY = ("lev", "tile", "sec")
HIGH = lax.Precision.HIGHEST
MESH = pl.DeviceIdType.MESH
BF = jnp.bfloat16
F32 = jnp.float32
NLEV, NLON, LANES = 64, 360, 384
TILES, GROUP, PLANE = 64, 8, 32
GROWS = 784
PART = (512, 272)
SHARE = (48, 32)
SLAB = (16, 640)


def dot(a, b):
    return jnp.dot(a, b, preferred_element_type=F32)


def dot_last(a, b):
    return lax.dot_general(a, b, (((1,), (1,)), ((), ())), preferred_element_type=F32)


def kernel(
    sent, consts, surface, cot_surface, land_sea, bias, w_in_h, w_mid_h, w_out_h,
    out_f, out_g, g_in, g_mid, g_out, g_bias,
    w_in, w_mid, w_out, w_in_t, w_mid_t, w_out_t, sv, cv, mv, bv, flat, bmat,
    pre, hgt, dbr, a_s, b_s, ra, rb, hs, hr, st, br, xs, a1, a2, s1, s2, inc, ginc,
    f_s, f_r, o_s, o_r, gacc, gs0, gs1, gr0, gr1, near0, near1, far0, far1, ag0, ag1,
    sems, hsem, wsem,
):
    lev, tile, sec = (lax.axis_index(a) for a in EVERY)
    r = lax.rem(lev, 2)
    me_g = lev * 2 + sec
    spot = lax.rem(tile, 8)
    z_lo = lax.div(tile, 8)
    core = lax.rem(spot, 2)
    me_c = lev * 4 + lax.div(spot, 2)
    me_p = core * 16 + me_c
    mate = (lev, tile + 1 - 2 * core, sec)
    pos = lax.rem(z_lo, 4)
    quad = lax.div(z_lo, 4)
    me_f = sec * 2 + quad
    sample = lax.div(lev, 2) * 2 + sec
    gs, gr, near, far, ag = (gs0, gs1), (gr0, gr1), (near0, near1), (far0, far1), (ag0, ag1)

    def of_group(q):
        return (lax.div(q, 2), tile, lax.rem(q, 2))

    def of_plane(q):
        chip = lax.rem(q, 16)
        return (lax.div(chip, 4), z_lo * 8 + lax.rem(chip, 4) * 2 + lax.div(q, 16), sec)

    def of_near(q):
        return (lev, (quad * 4 + q) * 8 + spot, sec)

    def of_far(q):
        return (lev, (lax.rem(q, 2) * 4 + pos) * 8 + spot, lax.div(q, 2))

    above = (lev + 1 - 2 * r, lax.rem(tile + r, TILES), sec)
    below_dev = (lev + 1 - 2 * r, lax.rem(tile + TILES - 1 + r, TILES), sec)

    fetches = [
        pltpu.make_async_copy(src, dst, wsem.at[i])
        for i, (src, dst) in enumerate(
            (
                (surface.at[sample], sv), (cot_surface.at[sample], cv), (land_sea, mv), (bias, bv),
                (w_in_h, w_in), (w_mid_h, w_mid), (w_out_h, w_out_t),
            )
        )
    ]
    for copy in fetches:
        copy.start()

    barrier = pltpu.get_barrier_semaphore()

    def greet(where):
        pl.semaphore_signal(barrier, inc=1, device_id=where, device_id_type=MESH)

    def each(n, me, act):
        def go(p, c):
            act(lax.rem(me + p, n))
            return c

        lax.fori_loop(1, n, go, 0)

    each(GROUP, me_g, lambda q: greet(of_group(q)))
    greet(above)
    greet(below_dev)
    each(PLANE, me_p, lambda q: greet(of_plane(q)))
    each(4, pos, lambda q: greet(of_near(q)))
    each(4, me_f, lambda q: greet(of_far(q)))

    def pack(dst, g, uv, t, rest):
        dst[g, :, 0:384] = uv.astype(BF)
        dst[g, :, 384:512] = jnp.concatenate([t[:, 0:128], t[:, 256:384]], axis=0).astype(BF)
        dst[g, :, 512:640] = jnp.concatenate([t[:, 128:256], rest], axis=0).astype(BF)

    def unpack(slab):
        uv, one, two = slab[:, 0:384], slab[:, 384:512], slab[:, 512:640]
        t = jnp.concatenate([one[0:8], two[0:8], one[8:16]], axis=1)
        return uv[0:8], uv[8:16], t, two[8:16]

    nothing = jnp.zeros((8, 128), F32)
    for g in range(GROUP):
        for base, dst in ((0, a_s), (24, b_s)):
            wide = sent[g, base : base + 24, :].astype(F32)
            pack(dst, g, wide[0:16], wide[16:24], nothing)
    pl.semaphore_wait(barrier, GROUP - 1 + 2 + PLANE - 1 + 3 + 3)

    def push(src, dst, k, where):
        pushed.add(k)
        pltpu.make_async_remote_copy(
            src_ref=src, dst_ref=dst, send_sem=sems.at[2 * k], recv_sem=sems.at[2 * k + 1],
            device_id=where, device_id_type=MESH,
        ).start()

    def finish(ref, sem):
        pltpu.make_async_copy(ref, ref, sem).wait()

    pushed, taken, halos_sent, halos_taken = set(), set(), set(), set()

    def done(ref, i):
        taken.add(i)
        finish(ref, sems.at[i])

    def leave():
        sizes = (
            ra.at[pl.ds(0, 7)], rb.at[pl.ds(0, 7)], f_r.at[pl.ds(0, 7)], o_r.at[pl.ds(0, 7)],
            gr0.at[pl.ds(0, PLANE - 1)], gr1.at[pl.ds(0, PLANE - 1)], near0.at[pl.ds(0, 3)], near1.at[pl.ds(0, 3)],
            far0.at[pl.ds(0, 3)], far1.at[pl.ds(0, 3)],
            ag0.at[pl.ds(0, 15 * SHARE[0])], ag1.at[pl.ds(0, 15 * SHARE[1])],
            ag0.at[pl.ds(0, 16 * SHARE[0])], ag1.at[pl.ds(0, 16 * SHARE[1])],
        )
        for k in sorted(pushed):
            done(sizes[k], 2 * k)
            if 2 * k + 1 not in taken:
                done(sizes[k], 2 * k + 1)
        for k in sorted(halos_sent):
            for way in (0, 1):
                finish(hs.at[k], hsem.at[k, way, 0])
                if k not in halos_taken:
                    finish(hr.at[k, way], hsem.at[k, way, 1])

    each(GROUP, me_g, lambda q: push(a_s.at[q], ra.at[me_g], 0, of_group(q)))
    each(GROUP, me_g, lambda q: push(b_s.at[q], rb.at[me_g], 1, of_group(q)))

    lane = lax.broadcasted_iota(jnp.int32, (64, LANES), 1)
    real = lane < NLON
    level = lax.broadcasted_iota(jnp.int32, (64, LANES), 0).astype(F32)
    weight = 1.0 / (level + 1.0)
    row_i = lax.broadcasted_iota(jnp.int32, (64, 192), 0)
    col_i = lax.broadcasted_iota(jnp.int32, (64, 192), 1)
    col_i = jnp.where(col_i >= 128, col_i - 128, jnp.where(col_i >= 64, col_i - 64, col_i))
    tri_rise = jnp.where(row_i >= col_i, 1.0, 0.0).astype(BF)
    tri_fall = jnp.where(row_i <= col_i, 1.0, 0.0).astype(BF)
    x_factor, sin_lat = consts[0:1, :], consts[1:2, :]
    has_before, has_after = consts[2:3, :] > 0, consts[3:4, :] > 0

    def vertical(which, values):
        one = values.astype(BF)
        rest = values - one.astype(F32)
        two = rest.astype(BF)
        three = (rest - two.astype(F32)).astype(BF)
        return dot(which, jnp.concatenate([one, two, three], axis=0))

    def rising(values):
        return vertical(tri_rise, values)

    def falling(values):
        return vertical(tri_fall, values)

    def dx(values):
        rows = values.shape[0]
        ln = lax.broadcasted_iota(jnp.int32, (rows, LANES), 1)
        full = jnp.where(ln == NLON, pltpu.roll(values, NLON, 1), values)
        full = jnp.where(ln == LANES - 1, pltpu.roll(values, LANES - NLON, 1), full)
        return (pltpu.roll(full, LANES - 1, 1) - pltpu.roll(full, 1, 1)) * x_factor

    def halo_send(k, first, second):
        halos_sent.add(k)
        hs[k, 0:64, :] = first.astype(BF)
        hs[k, 64:128, :] = second.astype(BF)
        for way, where in ((0, above), (1, below_dev)):
            pltpu.make_async_remote_copy(
                src_ref=hs.at[k], dst_ref=hr.at[k, way], send_sem=hsem.at[k, way, 0],
                recv_sem=hsem.at[k, way, 1], device_id=where, device_id_type=MESH,
            ).start()

    def halo_take(k):
        halos_taken.add(k)
        for way in (0, 1):
            finish(hr.at[k, way], hsem.at[k, way, 1])
        before, after = hr[k, 0].astype(F32), hr[k, 1].astype(F32)
        zero = jnp.zeros((), F32)
        diff = (jnp.where(has_after, after, zero) - jnp.where(has_before, before, zero)) * 0.5
        return diff[0:64], diff[64:128]

    def forward(k):
        pre[...] = dot(w_in_t[...], xs[k, 0:192, :])
        keep(a1, s1, k, True)
        pre[...] = dot(w_mid_t[...], a1[k])
        keep(a2, s2, k, False)
        return dot(w_out_t[...], a2[k]).astype(BF).astype(F32)

    def keep(act, slope, k, biased):
        def block(i, c):
            rows = pl.ds(pl.multiple_of(i * 32, 32), 32)
            value = pre[rows, :] + bmat[rows, :] if biased else pre[rows, :]
            cumulative = 0.5 * (1.0 + lax.erf(value * INV_SQRT_TWO))
            density = jnp.exp(-0.5 * value * value) * INV_SQRT_TWO_PI
            act[k, rows, :] = (value * cumulative).astype(BF)
            slope[k, rows, :] = cumulative + value * density
            return c

        lax.fori_loop(0, 12, block, 0)

    def backward(k, tend_bar):
        second_bar = (dot(w_out[...], tend_bar) * s2[k]).astype(BF)
        first_bar = (dot(w_mid[...], second_bar) * s1[k]).astype(BF)
        return second_bar, first_bar, dot(w_in[...], first_bar).astype(BF).astype(F32)

    def gradients(k, tend_bar, second_bar, first_bar):
        return (
            (0, dot_last(tend_bar, a2[k])),
            (192, dot_last(a1[k], second_bar)),
            (576, dot_last(xs[k], first_bar)),
        )

    def dynamics(dv, dh):
        u, v = st[0:64, :], st[64:128, :]
        div = dx(u) + dv
        flux = rising(div) * (1.0 / NLEV)
        return (
            -dx(hgt[...]) + sin_lat * v, -dh - sin_lat * u, -flux,
            jnp.sum(div, axis=0, keepdims=True) * (-1.0 / NLEV),
        )

    def div_bar(surf_bar):
        return (-falling(br[128:192, :]) - surf_bar) * (1.0 / NLEV)

    def adjoint(da, ddb):
        a_u, a_v = br[0:64, :], br[64:128, :]
        hb = dx(a_u) + da
        return (
            -dx(dbr[...]) - sin_lat * a_v, -ddb + sin_lat * a_u, weight * rising(hb),
            jnp.sum(hb, axis=0, keepdims=True),
        )

    def give(src, change, surf_change, dst, k):
        high = surf_change.astype(BF)
        low = (surf_change - high.astype(F32)).astype(BF)
        rows = lax.broadcasted_iota(jnp.int32, (8, 128), 0)
        tail = nothing
        for i in range(6):
            block = (high, low)[i // 3].astype(F32)[:, 128 * (i % 3) : 128 * (i % 3) + 128]
            tail = jnp.where(rows == i, block, tail)
        for g in range(GROUP):
            u, v, t = (change[f * 64 + g * 8 : f * 64 + g * 8 + 8, :] for f in range(3))
            pack(src, g, jnp.concatenate([u, v], axis=0), t, tail)
        dst[me_g] = src[me_g]
        each(GROUP, me_g, lambda q: push(src.at[q], dst.at[me_g], k, of_group(q)))

    ra[me_g] = a_s[me_g]
    rb[me_g] = b_s[me_g]
    for copy in fetches:
        copy.wait()
    flat[...] = jnp.zeros_like(flat)
    flat[0:1, 0:NLON] = jnp.where(r == 0, sv[0:1, :], sv[1:2, :])
    flat[1:2, 0:NLON] = TIME_STEP * jnp.where(r == 0, cv[0:1, :], cv[1:2, :])
    flat[2:3, 0:NLON] = jnp.where(jnp.where(r == 0, mv[0:1, :], mv[1:2, :]) > 0, 1.0, 0.0)
    land = flat[2:3, :] > 0
    mask_row = lax.broadcasted_iota(jnp.int32, (16, LANES), 0)
    sea_or_land = jnp.where(land, 1, 0)
    hot = jnp.where((mask_row == sea_or_land) & (lax.broadcasted_iota(jnp.int32, (16, LANES), 1) < NLON), 1.0, 0.0)
    xs[0, 192:208, :] = hot.astype(BF)
    xs[1, 192:208, :] = hot.astype(BF)
    bias_row = lax.broadcasted_iota(jnp.int32, (8, 384), 0)
    both = jnp.where(bias_row == 0, bv[0:1, :], jnp.where(bias_row == 1, bv[1:2, :], 0.0))
    bmat[...] = lax.dot_general(both, hot[0:8], (((0,), (0,)), ((), ())), precision=HIGH, preferred_element_type=F32)
    w_in_t[...] = w_in[...].T
    w_mid_t[...] = w_mid[...].T
    w_out[...] = w_out_t[...].T
    surf0, sbar0 = flat[0:1, :], flat[1:2, :]

    done(ra.at[pl.ds(0, 7)], 1)
    for g in range(GROUP):
        u, v, t, _ = unpack(ra[g].astype(F32))
        for f, part in enumerate((u, v, t)):
            st[f * 64 + g * 8 : f * 64 + g * 8 + 8, :] = part
    hgt[...] = falling(weight * st[128:192, :]) + surf0
    halo_send(0, st[64:128, :], hgt[...])
    xs[0, 0:192, :] = st[...].astype(BF)
    tend = forward(0)

    done(rb.at[pl.ds(0, 7)], 3)
    for g in range(GROUP):
        u, v, t, _ = unpack(rb[g].astype(F32))
        for f, part in enumerate((u, v, t)):
            br[f * 64 + g * 8 : f * 64 + g * 8 + 8, :] = part
    dbr[...] = div_bar(sbar0)
    halo_send(1, br[64:128, :], dbr[...])

    du, dv, dt, dsurf = dynamics(*halo_take(0))
    for i, d in enumerate((du, dv, dt)):
        at = slice(64 * i, 64 * i + 64)
        change = TIME_STEP * (d + tend[at])
        inc[at, :] = change
        st[at, :] = st[at, :] + change
    surf_inc = TIME_STEP * dsurf
    surf1 = surf0 + surf_inc
    hgt[...] = falling(weight * st[128:192, :]) + surf1
    halo_send(2, st[64:128, :], hgt[...])
    xs[1, 0:192, :] = st[...].astype(BF)
    tend = forward(1)

    t0 = br[...].astype(BF)
    second_bar, first_bar, input_bar = backward(1, t0)
    au, av, at_, asurf = adjoint(*halo_take(1))
    for i, d in enumerate((au, av, at_)):
        at = slice(64 * i, 64 * i + 64)
        change = d + input_bar[at]
        ginc[at, :] = change
        br[at, :] = jnp.where(real, br[at, :] + TIME_STEP * change, 0.0)
    gsurf = asurf
    sbar1 = sbar0 + TIME_STEP * asurf
    dbr[...] = div_bar(sbar1)
    halo_send(3, br[64:128, :], dbr[...])

    du, dv, dt, dsurf = dynamics(*halo_take(2))
    for i, d in enumerate((du, dv, dt)):
        at = slice(64 * i, 64 * i + 64)
        inc[at, :] = inc[at, :] + TIME_STEP * (d + tend[at])
    give(f_s, inc, surf_inc + TIME_STEP * dsurf, f_r, 2)

    for at, g in gradients(1, t0, second_bar, first_bar):
        gacc[at : at + g.shape[0], :] = g

    def share(ref, q, part):
        return ref.at[pl.ds(pl.multiple_of(q * SHARE[part], 16), SHARE[part])]

    def stage(total, at, part):
        for b in range(3):
            base = PART[part] * b + at
            gs[part][base : base + total.shape[0], :] = total[:, 128 * b : 128 * b + 128].astype(BF)

    def scatter(part):
        each(PLANE, me_p, lambda q: push(share(gs[part], q, part), gr[part].at[me_p], 4 + part, of_plane(q)))

    gs1[3 * PART[1] :, :] = jnp.zeros((PLANE * SHARE[1] - 3 * PART[1], 128), BF)
    t1 = br[...].astype(BF)
    second_bar = (dot(w_out[...], t1) * s2[0]).astype(BF)
    stage(gacc[0:192, :] + dot_last(t1, a2[0]), 0, 0)
    mid = gacc[192:576, :] + dot_last(a1[0], second_bar)
    stage(mid[0:320], 192, 0)
    stage(mid[320:384], 0, 1)
    scatter(0)
    first_bar = (dot(w_mid[...], second_bar) * s1[0]).astype(BF)
    stage(gacc[576:784, :] + dot_last(xs[0], first_bar), 64, 1)
    scatter(1)
    input_bar = dot(w_in[...], first_bar).astype(BF).astype(F32)

    au, av, at_, asurf = adjoint(*halo_take(3))
    for i, d in enumerate((au, av, at_)):
        at = slice(64 * i, 64 * i + 64)
        ginc[at, :] = ginc[at, :] + d + input_bar[at]
    give(o_s, ginc, gsurf + asurf, o_r, 3)

    def sum_plane(part):
        done(gr[part].at[pl.ds(0, PLANE - 1)], 2 * (4 + part) + 1)
        mine = gs[part][pl.ds(pl.multiple_of(me_p * SHARE[part], 16), SHARE[part]), :].astype(F32)
        near[part][pos] = lax.fori_loop(
            1, PLANE, lambda p, acc: acc + gr[part][lax.rem(me_p + p, PLANE)].astype(F32), mine
        )
        each(4, pos, lambda q: push(near[part].at[pos], near[part].at[pos], 6 + part, of_near(q)))

    def sum_near(part):
        done(near[part].at[pl.ds(0, 3)], 2 * (6 + part) + 1)
        n = near[part]
        far[part][me_f] = ((n[0] + n[1]) + (n[2] + n[3])).astype(BF)
        each(4, me_f, lambda q: push(far[part].at[me_f], far[part].at[me_f], 8 + part, of_far(q)))

    def sum_far(part):
        done(far[part].at[pl.ds(0, 3)], 2 * (8 + part) + 1)
        f = [far[part][i].astype(F32) for i in range(4)]
        at = pl.ds(pl.multiple_of(me_p * SHARE[part], 16), SHARE[part])
        ag[part][at, :] = ((f[0] + f[1]) + (f[2] + f[3])).astype(BF)
        own = share(ag[part], me_p, part)
        each(16, me_c, lambda q: push(own, own, 10 + part, of_plane(core * 16 + q)))

    def to_mate(part):
        done(ag[part].at[pl.ds(0, 15 * SHARE[part])], 2 * (10 + part) + 1)
        rows = 16 * SHARE[part]
        half = ag[part].at[pl.ds(pl.multiple_of(core * rows, 16), rows)]
        push(half, half, 12 + part, mate)

    sum_plane(0)
    sum_plane(1)
    sum_near(0)
    sum_near(1)
    sum_far(0)
    sum_far(1)

    def columns_out(came, out):
        for g in range(GROUP):
            u, v, t, rest = unpack(came[g].astype(F32))
            high = jnp.concatenate([rest[0:1], rest[1:2], rest[2:3]], axis=1)
            low = jnp.concatenate([rest[3:4], rest[4:5], rest[5:6]], axis=1)
            row = lax.broadcasted_iota(jnp.int32, (8, LANES), 0)
            tail = jnp.where(row == 0, high, jnp.where(row == 1, low, 0.0))
            out[g] = jnp.concatenate([u, v, t, tail], axis=0).astype(BF)

    to_mate(0)
    done(f_r.at[pl.ds(0, 7)], 5)
    columns_out(f_r, out_f)
    to_mate(1)
    done(o_r.at[pl.ds(0, 7)], 7)
    columns_out(o_r, out_g)

    def taken_from(part, b, first, last):
        base = PART[part] * b
        return ag[part][base + first : base + last, :].astype(F32)

    done(ag0.at[pl.ds(0, 16 * SHARE[0])], 25)
    for b in range(3):
        lanes = slice(128 * b, 128 * b + 128)
        g_out[:, lanes] = taken_from(0, b, 0, 192)
        g_mid[0:320, lanes] = taken_from(0, b, 192, 512)
    done(ag1.at[pl.ds(0, 16 * SHARE[1])], 27)
    for b in range(3):
        lanes = slice(128 * b, 128 * b + 128)
        g_mid[320:384, lanes] = taken_from(1, b, 0, 64)
        g_in[:, lanes] = taken_from(1, b, 64, 256)
        g_bias[:, lanes] = taken_from(1, b, 256, 272)[0:2]
    leave()


def call(*operands):
    def v(shape, dtype):
        return pltpu.VMEM(shape, dtype)

    slab = (GROUP, *SLAB)
    hidden = (2, 384, LANES)
    hbm, vmem = pl.BlockSpec(memory_space=pl.ANY), pl.BlockSpec(memory_space=pltpu.VMEM)
    return pl.pallas_call(
        kernel,
        out_shape=(
            jax.ShapeDtypeStruct((GROUP, 32, LANES), BF),
            jax.ShapeDtypeStruct((GROUP, 32, LANES), BF),
            jax.ShapeDtypeStruct((192, 384), F32),
            jax.ShapeDtypeStruct((384, 384), F32),
            jax.ShapeDtypeStruct((192, 384), F32),
            jax.ShapeDtypeStruct((2, 384), F32),
        ),
        in_specs=[vmem] * 2 + [hbm] * 7,
        out_specs=tuple([vmem] * 6),
        scratch_shapes=[
            v((192, 384), BF), v((384, 384), BF), v((384, 192), BF),
            v((384, 192), BF), v((384, 384), BF), v((192, 384), BF),
            v((2, NLON), F32), v((2, NLON), F32), v((2, NLON), jnp.int32), v((2, 384), F32),
            v((8, LANES), F32), v((384, LANES), F32),
            v((384, LANES), F32), v((64, LANES), F32), v((64, LANES), F32),
            v(slab, BF), v(slab, BF), v(slab, BF), v(slab, BF),
            v((4, 128, LANES), BF), v((4, 2, 128, LANES), BF),
            v((192, LANES), F32), v((192, LANES), F32), v((2, 208, LANES), BF),
            v(hidden, BF), v(hidden, BF), v(hidden, F32), v(hidden, F32),
            v((192, LANES), F32), v((192, LANES), F32),
            v(slab, BF), v(slab, BF), v(slab, BF), v(slab, BF),
            v((GROWS, 384), F32),
            v((PLANE * SHARE[0], 128), BF), v((PLANE * SHARE[1], 128), BF),
            v((PLANE, SHARE[0], 128), BF), v((PLANE, SHARE[1], 128), BF),
            v((4, SHARE[0], 128), F32), v((4, SHARE[1], 128), F32),
            v((4, SHARE[0], 128), BF), v((4, SHARE[1], 128), BF),
            v((PLANE * SHARE[0], 128), BF), v((PLANE * SHARE[1], 128), BF),
            pltpu.SemaphoreType.DMA((28,)), pltpu.SemaphoreType.DMA((4, 2, 2)), pltpu.SemaphoreType.DMA((7,)),
        ],
        compiler_params=pltpu.CompilerParams(
            collective_id=0, has_side_effects=True, vmem_limit_bytes=40 * 2**20
        ),
        name="window",
    )(*operands)


def on_device(fields, surface, cot_fields, cot_surface, land_sea, w_in, w_mid, w_out, bias_in):
    lev_i, tile_i = lax.axis_index("lev"), lax.axis_index("tile")
    row_in_band = lax.rem(lev_i, 2)
    row = tile_i * 2 + row_in_band
    latitude = -0.5 * math.pi + (row.astype(F32) + 0.5) * (math.pi / (2 * TILES))
    x_factor = 0.5 / jnp.maximum(jnp.cos(latitude), COS_FLOOR)
    sin_lat = jnp.sin(latitude)

    def pad(values):
        return jnp.pad(values, [(0, 0)] * (values.ndim - 1) + [(0, LANES - NLON)])

    def to_columns(values):
        split = values.astype(BF).reshape(3, 8, 2, 2, 2, NLON)
        return pad(split.transpose(2, 4, 3, 0, 1, 5).reshape(8, 24, NLON))

    sent = jnp.concatenate([to_columns(fields), to_columns(TIME_STEP * cot_fields)], axis=1)
    consts = jnp.stack([x_factor, sin_lat, (row > 0).astype(F32), (row < 2 * TILES - 1).astype(F32)])
    consts = jnp.broadcast_to(jnp.concatenate([consts, consts])[:, None], (8, LANES))
    came_f, came_g, g_in, g_mid, g_out, g_bias = call(
        sent, consts, surface, cot_surface, land_sea, bias_in, w_in, w_mid, w_out.T
    )

    def returned(came):
        came = came[:, :, :NLON].astype(F32)
        levels = came[:, :24].reshape(2, 2, 2, 3, 8, NLON).transpose(3, 4, 0, 2, 1, 5).reshape(3, 8, 4, 2, NLON)
        level_flat = (came[:, 24] + came[:, 25]).reshape(2, 2, 2, NLON).transpose(0, 2, 1, 3).reshape(4, 2, NLON)
        return levels, level_flat

    df, ds = returned(came_f)
    dg, dgs = returned(came_g)
    return (
        fields + df,
        surface + ds,
        cot_fields + dg,
        cot_surface + dgs,
        g_in,
        g_mid,
        g_out.T,
        g_bias,
    )


def solution(mesh):
    levels = P(None, ("lev", "sec"), None, "tile", None)
    flat = P(None, "tile", None)
    return jax.shard_map(
        on_device,
        mesh=mesh,
        in_specs=(levels, flat, levels, flat, P("tile", None), P(), P(), P(), P()),
        out_specs=(levels, flat, levels, flat, P(), P(), P(), P()),
        check_vma=False,
    )
```

```python
import functools
import math

import jax
import jax.numpy as jnp
from jax import lax
from jax.experimental import pallas as pl
from jax.experimental.pallas import tpu as pltpu
from jax.sharding import PartitionSpec as P

TIME_STEP = 0.1
COS_FLOOR = 0.2
INV_SQRT_TWO = 1.0 / math.sqrt(2.0)
INV_SQRT_TWO_PI = 1.0 / math.sqrt(2.0 * math.pi)
EVERY = ("lev", "tile", "sec")
HIGH = lax.Precision.HIGHEST
MESH = pl.DeviceIdType.MESH
BF = jnp.bfloat16
F32 = jnp.float32
NLEV, NLON, LANES = 64, 360, 384
TILES, GROUP, PLANE = 64, 8, 32
GROWS = 784
PART = (512, 272)
SHARE = (48, 32)
SLAB = (16, 640)


def dot(a, b):
    return jnp.dot(a, b, preferred_element_type=F32)


def dot_last(a, b):
    return lax.dot_general(a, b, (((1,), (1,)), ((), ())), preferred_element_type=F32)


def row_of(lev, tile):
    return lax.rem(lev + lax.rem(tile, 2), 2)


def sample_half(lev, tile):
    flip = lax.rem(tile, 2) * (1 - lax.rem(lev, 2))
    return lax.rem(lax.div(lev, 2) + lax.rem(lax.div(tile, 2), 2) + flip, 2)


def kernel(
    sent, consts, surface, cot_surface, land_sea, bias, w_in_h, w_mid_h, w_out_h,
    out_f, out_g, g_in, g_mid, g_out, g_bias,
    w_in, w_mid, w_out, w_in_t, w_mid_t, w_out_t, sv, cv, mv, bv, flat, bmat,
    pre, hgt, dbr, a_s, b_s, ra, rb, hs, hr, st, br, xs, a1, a2, s1, s2, inc, ginc,
    f_s, f_r, o_s, o_r, gacc, gs0, gs1, mr0, mr1, cs0, cs1, gr0, gr1, near0, near1, far0, far1, ag0, ag1,
    sems, hsem, wsem,
):
    lev, tile, sec = (lax.axis_index(a) for a in EVERY)
    r = row_of(lev, tile)
    me_g = lev * 2 + sec
    spot = lax.rem(tile, 8)
    z_lo = lax.div(tile, 8)
    core = lax.rem(spot, 2)
    me_c = lev * 4 + lax.div(spot, 2)
    me_p = core * 16 + me_c
    mate = (lev, tile + 1 - 2 * core, sec)
    pos = lax.rem(z_lo, 4)
    quad = lax.div(z_lo, 4)
    me_f = sec * 2 + quad
    half_of = sample_half(lev, tile)
    sample = half_of * 2 + sec
    my_slot = (half_of * 2 + r) * 2 + sec
    gs, mr, cs, gr, near, far, ag = (gs0, gs1), (mr0, mr1), (cs0, cs1), (gr0, gr1), (near0, near1), (far0, far1), (ag0, ag1)

    def of_group(q):
        return (lax.div(q, 2), tile, lax.rem(q, 2))

    def of_plane(q):
        chip = lax.rem(q, 16)
        return (lax.div(chip, 4), z_lo * 8 + lax.rem(chip, 4) * 2 + lax.div(q, 16), sec)

    def of_near(q):
        return (lev, (quad * 4 + q) * 8 + spot, sec)

    def of_far(q):
        return (lev, (lax.rem(q, 2) * 4 + pos) * 8 + spot, lax.div(q, 2))

    def slot(q):
        their = lax.div(q, 2)
        return (sample_half(their, tile) * 2 + row_of(their, tile)) * 2 + lax.rem(q, 2)

    partner = lax.rem(lev + 5 - 2 * r, 4)
    above = (lev + (1 - r) * (partner - lev), lax.rem(tile + r, TILES), sec)
    below_dev = (lev + r * (partner - lev), lax.rem(tile + TILES - 1 + r, TILES), sec)

    fetches = [
        pltpu.make_async_copy(src, dst, wsem.at[i])
        for i, (src, dst) in enumerate(
            (
                (surface.at[sample], sv), (cot_surface.at[sample], cv), (land_sea, mv), (bias, bv),
                (w_in_h, w_in), (w_mid_h, w_mid), (w_out_h, w_out_t),
            )
        )
    ]
    for copy in fetches:
        copy.start()

    barrier = pltpu.get_barrier_semaphore()

    def greet(where):
        pl.semaphore_signal(barrier, inc=1, device_id=where, device_id_type=MESH)

    def each(n, me, act):
        def go(p, c):
            act(lax.rem(me + p, n))
            return c

        lax.fori_loop(1, n, go, 0)

    each(GROUP, me_g, lambda q: greet(of_group(q)))
    greet(above)
    greet(below_dev)
    each(16, me_c, lambda q: greet(of_plane(core * 16 + q)))
    greet(mate)
    each(4, pos, lambda q: greet(of_near(q)))
    each(4, me_f, lambda q: greet(of_far(q)))

    def pack(dst, g, uv, t, rest):
        dst[g, :, 0:384] = uv.astype(BF)
        dst[g, :, 384:512] = jnp.concatenate([t[:, 0:128], t[:, 256:384]], axis=0).astype(BF)
        dst[g, :, 512:640] = jnp.concatenate([t[:, 128:256], rest], axis=0).astype(BF)

    def unpack(slab):
        uv, one, two = slab[:, 0:384], slab[:, 384:512], slab[:, 512:640]
        t = jnp.concatenate([one[0:8], two[0:8], one[8:16]], axis=1)
        return uv[0:8], uv[8:16], t, two[8:16]

    nothing = jnp.zeros((8, 128), F32)
    for g in range(GROUP):
        for base, dst in ((0, a_s), (24, b_s)):
            wide = sent[g, base : base + 24, :].astype(F32)
            pack(dst, g, wide[0:16], wide[16:24], nothing)
    pl.semaphore_wait(barrier, GROUP - 1 + 2 + 15 + 1 + 3 + 3)

    def push(src, dst, k, where):
        pushed.add(k)
        pltpu.make_async_remote_copy(
            src_ref=src, dst_ref=dst, send_sem=sems.at[2 * k], recv_sem=sems.at[2 * k + 1],
            device_id=where, device_id_type=MESH,
        ).start()

    def finish(ref, sem):
        pltpu.make_async_copy(ref, ref, sem).wait()

    pushed, taken, halos_sent, halos_taken = set(), set(), set(), set()

    def done(ref, i):
        taken.add(i)
        finish(ref, sems.at[i])

    def leave():
        sizes = (
            ra.at[pl.ds(0, 7)], rb.at[pl.ds(0, 7)], f_r.at[pl.ds(0, 7)], o_r.at[pl.ds(0, 7)],
            mr0, mr1, near0.at[pl.ds(0, 3)], near1.at[pl.ds(0, 3)],
            far0.at[pl.ds(0, 3)], far1.at[pl.ds(0, 3)],
            ag0.at[pl.ds(0, 15 * SHARE[0])], ag1.at[pl.ds(0, 15 * SHARE[1])],
            ag0.at[pl.ds(0, 16 * SHARE[0])], ag1.at[pl.ds(0, 16 * SHARE[1])],
            gr0.at[pl.ds(0, 15)], gr1.at[pl.ds(0, 15)],
        )
        for k in sorted(pushed):
            done(sizes[k], 2 * k)
            if 2 * k + 1 not in taken:
                done(sizes[k], 2 * k + 1)
        for k in sorted(halos_sent):
            for way in (0, 1):
                finish(hs.at[k], hsem.at[k, way, 0])
                if k not in halos_taken:
                    finish(hr.at[k, way], hsem.at[k, way, 1])

    each(GROUP, me_g, lambda q: push(a_s.at[slot(q)], ra.at[me_g], 0, of_group(q)))
    each(GROUP, me_g, lambda q: push(b_s.at[slot(q)], rb.at[me_g], 1, of_group(q)))

    lane = lax.broadcasted_iota(jnp.int32, (64, LANES), 1)
    real = lane < NLON
    level = lax.broadcasted_iota(jnp.int32, (64, LANES), 0).astype(F32)
    weight = 1.0 / (level + 1.0)
    row_i = lax.broadcasted_iota(jnp.int32, (64, 192), 0)
    col_i = lax.broadcasted_iota(jnp.int32, (64, 192), 1)
    col_i = jnp.where(col_i >= 128, col_i - 128, jnp.where(col_i >= 64, col_i - 64, col_i))
    tri_rise = jnp.where(row_i >= col_i, 1.0, 0.0).astype(BF)
    tri_fall = jnp.where(row_i <= col_i, 1.0, 0.0).astype(BF)
    x_factor, sin_lat = consts[0:1, :], consts[1:2, :]
    has_before, has_after = consts[2:3, :] > 0, consts[3:4, :] > 0

    def vertical(which, values):
        one = values.astype(BF)
        rest = values - one.astype(F32)
        two = rest.astype(BF)
        three = (rest - two.astype(F32)).astype(BF)
        return dot(which, jnp.concatenate([one, two, three], axis=0))

    def rising(values):
        return vertical(tri_rise, values)

    def falling(values):
        return vertical(tri_fall, values)

    def dx(values):
        rows = values.shape[0]
        ln = lax.broadcasted_iota(jnp.int32, (rows, LANES), 1)
        full = jnp.where(ln == NLON, pltpu.roll(values, NLON, 1), values)
        full = jnp.where(ln == LANES - 1, pltpu.roll(values, LANES - NLON, 1), full)
        return (pltpu.roll(full, LANES - 1, 1) - pltpu.roll(full, 1, 1)) * x_factor

    def halo_send(k, first, second):
        halos_sent.add(k)
        hs[k, 0:64, :] = first.astype(BF)
        hs[k, 64:128, :] = second.astype(BF)
        for way, where in ((0, above), (1, below_dev)):
            pltpu.make_async_remote_copy(
                src_ref=hs.at[k], dst_ref=hr.at[k, way], send_sem=hsem.at[k, way, 0],
                recv_sem=hsem.at[k, way, 1], device_id=where, device_id_type=MESH,
            ).start()

    def halo_take(k):
        halos_taken.add(k)
        for way in (0, 1):
            finish(hr.at[k, way], hsem.at[k, way, 1])
        before, after = hr[k, 0].astype(F32), hr[k, 1].astype(F32)
        zero = jnp.zeros((), F32)
        diff = (jnp.where(has_after, after, zero) - jnp.where(has_before, before, zero)) * 0.5
        return diff[0:64], diff[64:128]

    def forward(k):
        pre[...] = dot(w_in_t[...], xs[k, 0:192, :])
        keep(a1, s1, k, True)
        pre[...] = dot(w_mid_t[...], a1[k])
        keep(a2, s2, k, False)
        return dot(w_out_t[...], a2[k]).astype(BF).astype(F32)

    def keep(act, slope, k, biased):
        def block(i, c):
            rows = pl.ds(pl.multiple_of(i * 32, 32), 32)
            value = pre[rows, :] + bmat[rows, :] if biased else pre[rows, :]
            cumulative = 0.5 * (1.0 + lax.erf(value * INV_SQRT_TWO))
            density = jnp.exp(-0.5 * value * value) * INV_SQRT_TWO_PI
            act[k, rows, :] = (value * cumulative).astype(BF)
            slope[k, rows, :] = cumulative + value * density
            return c

        lax.fori_loop(0, 12, block, 0)

    def backward(k, tend_bar):
        second_bar = (dot(w_out[...], tend_bar) * s2[k]).astype(BF)
        first_bar = (dot(w_mid[...], second_bar) * s1[k]).astype(BF)
        return second_bar, first_bar, dot(w_in[...], first_bar).astype(BF).astype(F32)

    def gradients(k, tend_bar, second_bar, first_bar):
        return (
            (0, dot_last(tend_bar, a2[k])),
            (192, dot_last(a1[k], second_bar)),
            (576, dot_last(xs[k], first_bar)),
        )

    def dynamics(dv, dh):
        u, v = st[0:64, :], st[64:128, :]
        div = dx(u) + dv
        flux = rising(div) * (1.0 / NLEV)
        return (
            -dx(hgt[...]) + sin_lat * v, -dh - sin_lat * u, -flux,
            jnp.sum(div, axis=0, keepdims=True) * (-1.0 / NLEV),
        )

    def div_bar(surf_bar):
        return (-falling(br[128:192, :]) - surf_bar) * (1.0 / NLEV)

    def adjoint(da, ddb):
        a_u, a_v = br[0:64, :], br[64:128, :]
        hb = dx(a_u) + da
        return (
            -dx(dbr[...]) - sin_lat * a_v, -ddb + sin_lat * a_u, weight * rising(hb),
            jnp.sum(hb, axis=0, keepdims=True),
        )

    def give(src, change, surf_change, dst, k):
        high = surf_change.astype(BF)
        low = (surf_change - high.astype(F32)).astype(BF)
        rows = lax.broadcasted_iota(jnp.int32, (8, 128), 0)
        tail = nothing
        for i in range(6):
            block = (high, low)[i // 3].astype(F32)[:, 128 * (i % 3) : 128 * (i % 3) + 128]
            tail = jnp.where(rows == i, block, tail)
        for g in range(GROUP):
            u, v, t = (change[f * 64 + g * 8 : f * 64 + g * 8 + 8, :] for f in range(3))
            pack(src, g, jnp.concatenate([u, v], axis=0), t, tail)
        dst[my_slot] = src[me_g]
        each(GROUP, me_g, lambda q: push(src.at[q], dst.at[my_slot], k, of_group(q)))

    ra[me_g] = a_s[my_slot]
    rb[me_g] = b_s[my_slot]
    for copy in fetches:
        copy.wait()
    flat[...] = jnp.zeros_like(flat)
    flat[0:1, 0:NLON] = jnp.where(r == 0, sv[0:1, :], sv[1:2, :])
    flat[1:2, 0:NLON] = TIME_STEP * jnp.where(r == 0, cv[0:1, :], cv[1:2, :])
    flat[2:3, 0:NLON] = jnp.where(jnp.where(r == 0, mv[0:1, :], mv[1:2, :]) > 0, 1.0, 0.0)
    land = flat[2:3, :] > 0
    mask_row = lax.broadcasted_iota(jnp.int32, (16, LANES), 0)
    sea_or_land = jnp.where(land, 1, 0)
    hot = jnp.where((mask_row == sea_or_land) & (lax.broadcasted_iota(jnp.int32, (16, LANES), 1) < NLON), 1.0, 0.0)
    xs[0, 192:208, :] = hot.astype(BF)
    xs[1, 192:208, :] = hot.astype(BF)
    bias_row = lax.broadcasted_iota(jnp.int32, (8, 384), 0)
    both = jnp.where(bias_row == 0, bv[0:1, :], jnp.where(bias_row == 1, bv[1:2, :], 0.0))
    bmat[...] = lax.dot_general(both, hot[0:8], (((0,), (0,)), ((), ())), precision=HIGH, preferred_element_type=F32)
    w_in_t[...] = w_in[...].T
    w_mid_t[...] = w_mid[...].T
    w_out[...] = w_out_t[...].T
    surf0, sbar0 = flat[0:1, :], flat[1:2, :]

    done(ra.at[pl.ds(0, 7)], 1)
    for g in range(GROUP):
        u, v, t, _ = unpack(ra[g].astype(F32))
        for f, part in enumerate((u, v, t)):
            st[f * 64 + g * 8 : f * 64 + g * 8 + 8, :] = part
    hgt[...] = falling(weight * st[128:192, :]) + surf0
    halo_send(0, st[64:128, :], hgt[...])
    xs[0, 0:192, :] = st[...].astype(BF)
    tend = forward(0)

    done(rb.at[pl.ds(0, 7)], 3)
    for g in range(GROUP):
        u, v, t, _ = unpack(rb[g].astype(F32))
        for f, part in enumerate((u, v, t)):
            br[f * 64 + g * 8 : f * 64 + g * 8 + 8, :] = part
    dbr[...] = div_bar(sbar0)
    halo_send(1, br[64:128, :], dbr[...])

    du, dv, dt, dsurf = dynamics(*halo_take(0))
    for i, d in enumerate((du, dv, dt)):
        at = slice(64 * i, 64 * i + 64)
        change = TIME_STEP * (d + tend[at])
        inc[at, :] = change
        st[at, :] = st[at, :] + change
    surf_inc = TIME_STEP * dsurf
    surf1 = surf0 + surf_inc
    hgt[...] = falling(weight * st[128:192, :]) + surf1
    halo_send(2, st[64:128, :], hgt[...])
    xs[1, 0:192, :] = st[...].astype(BF)
    tend = forward(1)

    t0 = br[...].astype(BF)
    second_bar, first_bar, input_bar = backward(1, t0)
    au, av, at_, asurf = adjoint(*halo_take(1))
    for i, d in enumerate((au, av, at_)):
        at = slice(64 * i, 64 * i + 64)
        change = d + input_bar[at]
        ginc[at, :] = change
        br[at, :] = jnp.where(real, br[at, :] + TIME_STEP * change, 0.0)
    gsurf = asurf
    sbar1 = sbar0 + TIME_STEP * asurf
    dbr[...] = div_bar(sbar1)
    halo_send(3, br[64:128, :], dbr[...])

    du, dv, dt, dsurf = dynamics(*halo_take(2))
    for i, d in enumerate((du, dv, dt)):
        at = slice(64 * i, 64 * i + 64)
        inc[at, :] = inc[at, :] + TIME_STEP * (d + tend[at])
    give(f_s, inc, surf_inc + TIME_STEP * dsurf, f_r, 2)

    for at, g in gradients(1, t0, second_bar, first_bar):
        gacc[at : at + g.shape[0], :] = g

    def share(ref, q, part):
        return ref.at[pl.ds(pl.multiple_of(q * SHARE[part], 16), SHARE[part])]

    def stage(total, at, part):
        for b in range(3):
            base = PART[part] * b + at
            gs[part][base : base + total.shape[0], :] = total[:, 128 * b : 128 * b + 128].astype(BF)

    def scatter(part):
        rows = 16 * SHARE[part]
        push(gs[part].at[pl.ds(pl.multiple_of((1 - core) * rows, 16), rows)], mr[part], 4 + part, mate)

    def combine(part):
        done(mr[part], 2 * (4 + part) + 1)
        rows = 16 * SHARE[part]
        own = gs[part][pl.ds(pl.multiple_of(core * rows, 16), rows), :].astype(F32)
        cs[part][...] = (own + mr[part][...].astype(F32)).astype(BF)
        each(16, me_c, lambda q: push(share(cs[part], q, part), gr[part].at[me_c], 14 + part, of_plane(core * 16 + q)))

    gs1[3 * PART[1] :, :] = jnp.zeros((PLANE * SHARE[1] - 3 * PART[1], 128), BF)
    t1 = br[...].astype(BF)
    second_bar = (dot(w_out[...], t1) * s2[0]).astype(BF)
    stage(gacc[0:192, :] + dot_last(t1, a2[0]), 0, 0)
    mid = gacc[192:576, :] + dot_last(a1[0], second_bar)
    stage(mid[0:320], 192, 0)
    stage(mid[320:384], 0, 1)
    scatter(0)
    first_bar = (dot(w_mid[...], second_bar) * s1[0]).astype(BF)
    stage(gacc[576:784, :] + dot_last(xs[0], first_bar), 64, 1)
    scatter(1)
    combine(0)
    input_bar = dot(w_in[...], first_bar).astype(BF).astype(F32)
    combine(1)

    au, av, at_, asurf = adjoint(*halo_take(3))
    for i, d in enumerate((au, av, at_)):
        at = slice(64 * i, 64 * i + 64)
        ginc[at, :] = ginc[at, :] + d + input_bar[at]
    give(o_s, ginc, gsurf + asurf, o_r, 3)

    def sum_plane(part):
        done(gr[part].at[pl.ds(0, 15)], 2 * (14 + part) + 1)
        mine = cs[part][pl.ds(pl.multiple_of(me_c * SHARE[part], 16), SHARE[part]), :].astype(F32)
        near[part][pos] = lax.fori_loop(
            1, 16, lambda p, acc: acc + gr[part][lax.rem(me_c + p, 16)].astype(F32), mine
        )
        each(4, pos, lambda q: push(near[part].at[pos], near[part].at[pos], 6 + part, of_near(q)))

    def sum_near(part):
        done(near[part].at[pl.ds(0, 3)], 2 * (6 + part) + 1)
        n = near[part]
        far[part][me_f] = (n[0] + n[1]) + (n[2] + n[3])
        each(4, me_f, lambda q: push(far[part].at[me_f], far[part].at[me_f], 8 + part, of_far(q)))

    def sum_far(part):
        done(far[part].at[pl.ds(0, 3)], 2 * (8 + part) + 1)
        f = far[part]
        at = pl.ds(pl.multiple_of(me_p * SHARE[part], 16), SHARE[part])
        ag[part][at, :] = ((f[0] + f[1]) + (f[2] + f[3])).astype(BF)
        own = share(ag[part], me_p, part)
        each(16, me_c, lambda q: push(own, own, 10 + part, of_plane(core * 16 + q)))

    def to_mate(part):
        done(ag[part].at[pl.ds(0, 15 * SHARE[part])], 2 * (10 + part) + 1)
        rows = 16 * SHARE[part]
        half = ag[part].at[pl.ds(pl.multiple_of(core * rows, 16), rows)]
        push(half, half, 12 + part, mate)

    sum_plane(0)
    sum_plane(1)
    sum_near(0)
    sum_near(1)
    sum_far(0)
    sum_far(1)

    def columns_out(came, out):
        for g in range(GROUP):
            u, v, t, rest = unpack(came[g].astype(F32))
            high = jnp.concatenate([rest[0:1], rest[1:2], rest[2:3]], axis=1)
            low = jnp.concatenate([rest[3:4], rest[4:5], rest[5:6]], axis=1)
            row = lax.broadcasted_iota(jnp.int32, (8, LANES), 0)
            tail = jnp.where(row == 0, high, jnp.where(row == 1, low, 0.0))
            out[g] = jnp.concatenate([u, v, t, tail], axis=0).astype(BF)

    to_mate(0)
    done(f_r.at[pl.ds(0, 7)], 5)
    columns_out(f_r, out_f)
    to_mate(1)
    done(o_r.at[pl.ds(0, 7)], 7)
    columns_out(o_r, out_g)

    def taken_from(part, b, first, last):
        base = PART[part] * b
        return ag[part][base + first : base + last, :].astype(F32)

    done(ag0.at[pl.ds(0, 16 * SHARE[0])], 25)
    for b in range(3):
        lanes = slice(128 * b, 128 * b + 128)
        g_out[:, lanes] = taken_from(0, b, 0, 192)
        g_mid[0:320, lanes] = taken_from(0, b, 192, 512)
    done(ag1.at[pl.ds(0, 16 * SHARE[1])], 27)
    for b in range(3):
        lanes = slice(128 * b, 128 * b + 128)
        g_mid[320:384, lanes] = taken_from(1, b, 0, 64)
        g_in[:, lanes] = taken_from(1, b, 64, 256)
        g_bias[:, lanes] = taken_from(1, b, 256, 272)[0:2]
    leave()


def call(*operands):
    def v(shape, dtype):
        return pltpu.VMEM(shape, dtype)

    slab = (GROUP, *SLAB)
    hidden = (2, 384, LANES)
    hbm, vmem = pl.BlockSpec(memory_space=pl.ANY), pl.BlockSpec(memory_space=pltpu.VMEM)
    return pl.pallas_call(
        kernel,
        out_shape=(
            jax.ShapeDtypeStruct((GROUP, 32, LANES), BF),
            jax.ShapeDtypeStruct((GROUP, 32, LANES), BF),
            jax.ShapeDtypeStruct((192, 384), F32),
            jax.ShapeDtypeStruct((384, 384), F32),
            jax.ShapeDtypeStruct((192, 384), F32),
            jax.ShapeDtypeStruct((2, 384), F32),
        ),
        in_specs=[vmem] * 2 + [hbm] * 7,
        out_specs=tuple([vmem] * 6),
        scratch_shapes=[
            v((192, 384), BF), v((384, 384), BF), v((384, 192), BF),
            v((384, 192), BF), v((384, 384), BF), v((192, 384), BF),
            v((2, NLON), F32), v((2, NLON), F32), v((2, NLON), jnp.int32), v((2, 384), F32),
            v((8, LANES), F32), v((384, LANES), F32),
            v((384, LANES), F32), v((64, LANES), F32), v((64, LANES), F32),
            v(slab, BF), v(slab, BF), v(slab, BF), v(slab, BF),
            v((4, 128, LANES), BF), v((4, 2, 128, LANES), BF),
            v((192, LANES), F32), v((192, LANES), F32), v((2, 208, LANES), BF),
            v(hidden, BF), v(hidden, BF), v(hidden, F32), v(hidden, F32),
            v((192, LANES), F32), v((192, LANES), F32),
            v(slab, BF), v(slab, BF), v(slab, BF), v(slab, BF),
            v((GROWS, 384), F32),
            v((PLANE * SHARE[0], 128), BF), v((PLANE * SHARE[1], 128), BF),
            v((16 * SHARE[0], 128), BF), v((16 * SHARE[1], 128), BF),
            v((16 * SHARE[0], 128), BF), v((16 * SHARE[1], 128), BF),
            v((16, SHARE[0], 128), BF), v((16, SHARE[1], 128), BF),
            v((4, SHARE[0], 128), F32), v((4, SHARE[1], 128), F32),
            v((4, SHARE[0], 128), F32), v((4, SHARE[1], 128), F32),
            v((PLANE * SHARE[0], 128), BF), v((PLANE * SHARE[1], 128), BF),
            pltpu.SemaphoreType.DMA((32,)), pltpu.SemaphoreType.DMA((4, 2, 2)), pltpu.SemaphoreType.DMA((7,)),
        ],
        compiler_params=pltpu.CompilerParams(
            collective_id=0, has_side_effects=True, vmem_limit_bytes=40 * 2**20
        ),
        name="window",
    )(*operands)


def on_device(fields, surface, cot_fields, cot_surface, land_sea, w_in, w_mid, w_out, bias_in):
    lev_i, tile_i = lax.axis_index("lev"), lax.axis_index("tile")
    row = tile_i * 2 + row_of(lev_i, tile_i)
    latitude = -0.5 * math.pi + (row.astype(F32) + 0.5) * (math.pi / (2 * TILES))
    x_factor = 0.5 / jnp.maximum(jnp.cos(latitude), COS_FLOOR)
    sin_lat = jnp.sin(latitude)

    def pad(values):
        return jnp.pad(values, [(0, 0)] * (values.ndim - 1) + [(0, LANES - NLON)])

    def to_columns(values):
        split = values.astype(BF).reshape(3, 8, 2, 2, 2, NLON)
        return pad(split.transpose(2, 4, 3, 0, 1, 5).reshape(8, 24, NLON))

    sent = jnp.concatenate([to_columns(fields), to_columns(TIME_STEP * cot_fields)], axis=1)
    consts = jnp.stack([x_factor, sin_lat, (row > 0).astype(F32), (row < 2 * TILES - 1).astype(F32)])
    consts = jnp.broadcast_to(jnp.concatenate([consts, consts])[:, None], (8, LANES))
    came_f, came_g, g_in, g_mid, g_out, g_bias = call(
        sent, consts, surface, cot_surface, land_sea, bias_in, w_in, w_mid, w_out.T
    )

    def returned(came):
        came = came[:, :, :NLON].astype(F32)
        levels = came[:, :24].reshape(2, 2, 2, 3, 8, NLON).transpose(3, 4, 0, 2, 1, 5).reshape(3, 8, 4, 2, NLON)
        level_flat = (came[:, 24] + came[:, 25]).reshape(2, 2, 2, NLON).transpose(0, 2, 1, 3).reshape(4, 2, NLON)
        return levels, level_flat

    df, ds = returned(came_f)
    dg, dgs = returned(came_g)
    return (
        fields + df,
        surface + ds,
        cot_fields + dg,
        cot_surface + dgs,
        g_in,
        g_mid,
        g_out.T,
        g_bias,
    )


def solution(mesh):
    levels = P(None, ("lev", "sec"), None, "tile", None)
    flat = P(None, "tile", None)
    return jax.shard_map(
        on_device,
        mesh=mesh,
        in_specs=(levels, flat, levels, flat, P("tile", None), P(), P(), P(), P()),
        out_specs=(levels, flat, levels, flat, P(), P(), P(), P()),
        check_vma=False,
    )
```

```python
import functools
import math

import jax
import jax.numpy as jnp
from jax import lax
from jax.experimental import pallas as pl
from jax.experimental.pallas import tpu as pltpu
from jax.sharding import PartitionSpec as P

TIME_STEP = 0.1
COS_FLOOR = 0.2
INV_SQRT_TWO = 1.0 / math.sqrt(2.0)
INV_SQRT_TWO_PI = 1.0 / math.sqrt(2.0 * math.pi)
EVERY = ("lev", "tile", "sec")
HIGH = lax.Precision.HIGHEST
MESH = pl.DeviceIdType.MESH
BF = jnp.bfloat16
F32 = jnp.float32
NLEV, NLON, LANES = 64, 360, 384
TILES, GROUP, PLANE = 64, 8, 32
GROWS = 784
PART = (512, 272)
SHARE = (48, 32)
SLAB = (16, 640)


def dot(a, b):
    return jnp.dot(a, b, preferred_element_type=F32)


def dot_last(a, b):
    return lax.dot_general(a, b, (((1,), (1,)), ((), ())), preferred_element_type=F32)


def row_of(lev, tile):
    return lax.rem(lev + lax.rem(tile, 2), 2)


def sample_half(lev, tile):
    flip = lax.rem(tile, 2) * (1 - lax.rem(lev, 2))
    return lax.rem(lax.div(lev, 2) + lax.rem(lax.div(tile, 2), 2) + flip, 2)


def kernel(
    sent, consts, surface, cot_surface, land_sea, bias, w_in_h, w_mid_h, w_out_h,
    out_f, out_g, g_in, g_mid, g_out, g_bias,
    w_in, w_mid, w_out, w_in_t, w_mid_t, w_out_t, sv, cv, mv, bv, flat, bmat,
    pre, hgt, dbr, a_s, b_s, ra, rb, hs, hr, st, br, xs, a1, a2, s1, s2, inc, ginc,
    f_s, f_r, o_s, o_r, gacc, gs0, gs1, mr0, mr1, cs0, cs1, gr0, gr1, near0, near1, far0, far1, ag0, ag1,
    sems, hsem, wsem,
):
    lev, tile, sec = (lax.axis_index(a) for a in EVERY)
    r = row_of(lev, tile)
    me_g = lev * 2 + sec
    spot = lax.rem(tile, 8)
    z_lo = lax.div(tile, 8)
    core = lax.rem(spot, 2)
    me_c = lev * 4 + lax.div(spot, 2)
    me_p = core * 16 + me_c
    mate = (lev, tile + 1 - 2 * core, sec)
    pos = lax.rem(z_lo, 4)
    quad = lax.div(z_lo, 4)
    me_f = sec * 2 + quad
    half_of = sample_half(lev, tile)
    sample = half_of * 2 + sec
    my_slot = (half_of * 2 + r) * 2 + sec
    gs, mr, cs, gr, near, far, ag = (gs0, gs1), (mr0, mr1), (cs0, cs1), (gr0, gr1), (near0, near1), (far0, far1), (ag0, ag1)

    def of_group(q):
        return (lax.div(q, 2), tile, lax.rem(q, 2))

    def of_plane(q):
        chip = lax.rem(q, 16)
        return (lax.div(chip, 4), z_lo * 8 + lax.rem(chip, 4) * 2 + lax.div(q, 16), sec)

    def of_near(q):
        return (lev, (quad * 4 + q) * 8 + spot, sec)

    def of_far(q):
        return (lev, (lax.rem(q, 2) * 4 + pos) * 8 + spot, lax.div(q, 2))

    def slot(q):
        their = lax.div(q, 2)
        return (sample_half(their, tile) * 2 + row_of(their, tile)) * 2 + lax.rem(q, 2)

    partner = lax.rem(lev + 5 - 2 * r, 4)
    above = (lev + (1 - r) * (partner - lev), lax.rem(tile + r, TILES), sec)
    below_dev = (lev + r * (partner - lev), lax.rem(tile + TILES - 1 + r, TILES), sec)

    fetches = [
        pltpu.make_async_copy(src, dst, wsem.at[i])
        for i, (src, dst) in enumerate(
            (
                (surface.at[sample], sv), (cot_surface.at[sample], cv), (land_sea, mv), (bias, bv),
                (w_in_h, w_in), (w_mid_h, w_mid), (w_out_h, w_out_t),
            )
        )
    ]
    for copy in fetches:
        copy.start()

    barrier = pltpu.get_barrier_semaphore()

    def greet(where):
        pl.semaphore_signal(barrier, inc=1, device_id=where, device_id_type=MESH)

    def each(n, me, act):
        def go(p, c):
            act(lax.rem(me + p, n))
            return c

        lax.fori_loop(1, n, go, 0)

    each(GROUP, me_g, lambda q: greet(of_group(q)))
    greet(above)
    greet(below_dev)
    each(16, me_c, lambda q: greet(of_plane(core * 16 + q)))
    greet(mate)
    each(4, pos, lambda q: greet(of_near(q)))
    each(4, me_f, lambda q: greet(of_far(q)))

    def pack(dst, g, uv, t, rest):
        dst[g, :, 0:384] = uv.astype(BF)
        dst[g, :, 384:512] = jnp.concatenate([t[:, 0:128], t[:, 256:384]], axis=0).astype(BF)
        dst[g, :, 512:640] = jnp.concatenate([t[:, 128:256], rest], axis=0).astype(BF)

    def unpack(slab):
        uv, one, two = slab[:, 0:384], slab[:, 384:512], slab[:, 512:640]
        t = jnp.concatenate([one[0:8], two[0:8], one[8:16]], axis=1)
        return uv[0:8], uv[8:16], t, two[8:16]

    nothing = jnp.zeros((8, 128), F32)
    for g in range(GROUP):
        for base, dst in ((0, a_s), (24, b_s)):
            wide = sent[g, base : base + 24, :].astype(F32)
            pack(dst, g, wide[0:16], wide[16:24], nothing)
    pl.semaphore_wait(barrier, GROUP - 1 + 2 + 15 + 1 + 3 + 3)

    def push(src, dst, k, where):
        pushed.add(k)
        pltpu.make_async_remote_copy(
            src_ref=src, dst_ref=dst, send_sem=sems.at[2 * k], recv_sem=sems.at[2 * k + 1],
            device_id=where, device_id_type=MESH,
        ).start()

    def finish(ref, sem):
        pltpu.make_async_copy(ref, ref, sem).wait()

    pushed, taken, halos_sent, halos_taken = set(), set(), set(), set()

    def done(ref, i):
        taken.add(i)
        finish(ref, sems.at[i])

    def leave():
        sizes = (
            ra.at[pl.ds(0, 7)], rb.at[pl.ds(0, 7)], f_r.at[pl.ds(0, 7)], o_r.at[pl.ds(0, 7)],
            mr0, mr1, near0.at[pl.ds(0, 3)], near1.at[pl.ds(0, 3)],
            far0.at[pl.ds(0, 3)], far1.at[pl.ds(0, 3)],
            ag0.at[pl.ds(0, 15 * SHARE[0])], ag1.at[pl.ds(0, 15 * SHARE[1])],
            ag0.at[pl.ds(0, 16 * SHARE[0])], ag1.at[pl.ds(0, 16 * SHARE[1])],
            gr0.at[pl.ds(0, 15)], gr1.at[pl.ds(0, 15)],
        )
        for k in sorted(pushed):
            done(sizes[k], 2 * k)
            if 2 * k + 1 not in taken:
                done(sizes[k], 2 * k + 1)
        for k in sorted(halos_sent):
            for way in (0, 1):
                finish(hs.at[k], hsem.at[k, way, 0])
                if k not in halos_taken:
                    finish(hr.at[k, way], hsem.at[k, way, 1])

    each(GROUP, me_g, lambda q: push(a_s.at[slot(q)], ra.at[me_g], 0, of_group(q)))
    each(GROUP, me_g, lambda q: push(b_s.at[slot(q)], rb.at[me_g], 1, of_group(q)))

    lane = lax.broadcasted_iota(jnp.int32, (64, LANES), 1)
    real = lane < NLON
    level = lax.broadcasted_iota(jnp.int32, (64, LANES), 0).astype(F32)
    weight = 1.0 / (level + 1.0)
    row_i = lax.broadcasted_iota(jnp.int32, (64, 192), 0)
    col_i = lax.broadcasted_iota(jnp.int32, (64, 192), 1)
    col_i = jnp.where(col_i >= 128, col_i - 128, jnp.where(col_i >= 64, col_i - 64, col_i))
    tri_rise = jnp.where(row_i >= col_i, 1.0, 0.0).astype(BF)
    tri_fall = jnp.where(row_i <= col_i, 1.0, 0.0).astype(BF)
    x_factor, sin_lat = consts[0:1, :], consts[1:2, :]
    has_before, has_after = consts[2:3, :] > 0, consts[3:4, :] > 0

    def vertical(which, values):
        one = values.astype(BF)
        rest = values - one.astype(F32)
        two = rest.astype(BF)
        three = (rest - two.astype(F32)).astype(BF)
        return dot(which, jnp.concatenate([one, two, three], axis=0))

    def rising(values):
        return vertical(tri_rise, values)

    def falling(values):
        return vertical(tri_fall, values)

    def dx(values):
        rows = values.shape[0]
        ln = lax.broadcasted_iota(jnp.int32, (rows, LANES), 1)
        full = jnp.where(ln == NLON, pltpu.roll(values, NLON, 1), values)
        full = jnp.where(ln == LANES - 1, pltpu.roll(values, LANES - NLON, 1), full)
        return (pltpu.roll(full, LANES - 1, 1) - pltpu.roll(full, 1, 1)) * x_factor

    def halo_send(k, first, second):
        halos_sent.add(k)
        hs[k, 0:64, :] = first.astype(BF)
        hs[k, 64:128, :] = second.astype(BF)
        for way, where in ((0, above), (1, below_dev)):
            pltpu.make_async_remote_copy(
                src_ref=hs.at[k], dst_ref=hr.at[k, way], send_sem=hsem.at[k, way, 0],
                recv_sem=hsem.at[k, way, 1], device_id=where, device_id_type=MESH,
            ).start()

    def halo_take(k):
        halos_taken.add(k)
        for way in (0, 1):
            finish(hr.at[k, way], hsem.at[k, way, 1])
        before, after = hr[k, 0].astype(F32), hr[k, 1].astype(F32)
        zero = jnp.zeros((), F32)
        diff = (jnp.where(has_after, after, zero) - jnp.where(has_before, before, zero)) * 0.5
        return diff[0:64], diff[64:128]

    def forward(k):
        pre[...] = dot(w_in_t[...], xs[k, 0:192, :])
        keep(a1, s1, k, True)
        pre[...] = dot(w_mid_t[...], a1[k])
        keep(a2, s2, k, False)
        return dot(w_out_t[...], a2[k]).astype(BF).astype(F32)

    def keep(act, slope, k, biased):
        def block(i, c):
            rows = pl.ds(pl.multiple_of(i * 32, 32), 32)
            value = pre[rows, :] + bmat[rows, :] if biased else pre[rows, :]
            cumulative = 0.5 * (1.0 + lax.erf(value * INV_SQRT_TWO))
            density = jnp.exp(-0.5 * value * value) * INV_SQRT_TWO_PI
            act[k, rows, :] = (value * cumulative).astype(BF)
            slope[k, rows, :] = cumulative + value * density
            return c

        lax.fori_loop(0, 12, block, 0)

    def backward(k, tend_bar):
        second_bar = (dot(w_out[...], tend_bar) * s2[k]).astype(BF)
        first_bar = (dot(w_mid[...], second_bar) * s1[k]).astype(BF)
        return second_bar, first_bar, dot(w_in[...], first_bar).astype(BF).astype(F32)

    def gradients(k, tend_bar, second_bar, first_bar):
        return (
            (0, dot_last(tend_bar, a2[k])),
            (192, dot_last(a1[k], second_bar)),
            (576, dot_last(xs[k], first_bar)),
        )

    def dynamics(dv, dh):
        u, v = st[0:64, :], st[64:128, :]
        div = dx(u) + dv
        flux = rising(div) * (1.0 / NLEV)
        return (
            -dx(hgt[...]) + sin_lat * v, -dh - sin_lat * u, -flux,
            jnp.sum(div, axis=0, keepdims=True) * (-1.0 / NLEV),
        )

    def div_bar(surf_bar):
        return (-falling(br[128:192, :]) - surf_bar) * (1.0 / NLEV)

    def adjoint(da, ddb):
        a_u, a_v = br[0:64, :], br[64:128, :]
        hb = dx(a_u) + da
        return (
            -dx(dbr[...]) - sin_lat * a_v, -ddb + sin_lat * a_u, weight * rising(hb),
            jnp.sum(hb, axis=0, keepdims=True),
        )

    def lay_out(src, change, surf_change, dst):
        high = surf_change.astype(BF)
        low = (surf_change - high.astype(F32)).astype(BF)
        rows = lax.broadcasted_iota(jnp.int32, (8, 128), 0)
        tail = nothing
        for i in range(6):
            block = (high, low)[i // 3].astype(F32)[:, 128 * (i % 3) : 128 * (i % 3) + 128]
            tail = jnp.where(rows == i, block, tail)
        for g in range(GROUP):
            u, v, t = (change[f * 64 + g * 8 : f * 64 + g * 8 + 8, :] for f in range(3))
            pack(src, g, jnp.concatenate([u, v], axis=0), t, tail)
        dst[my_slot] = src[me_g]

    def give(src, dst, k):
        each(GROUP, me_g, lambda q: push(src.at[q], dst.at[my_slot], k, of_group(q)))

    ra[me_g] = a_s[my_slot]
    rb[me_g] = b_s[my_slot]
    for copy in fetches:
        copy.wait()
    flat[...] = jnp.zeros_like(flat)
    flat[0:1, 0:NLON] = jnp.where(r == 0, sv[0:1, :], sv[1:2, :])
    flat[1:2, 0:NLON] = TIME_STEP * jnp.where(r == 0, cv[0:1, :], cv[1:2, :])
    flat[2:3, 0:NLON] = jnp.where(jnp.where(r == 0, mv[0:1, :], mv[1:2, :]) > 0, 1.0, 0.0)
    land = flat[2:3, :] > 0
    mask_row = lax.broadcasted_iota(jnp.int32, (16, LANES), 0)
    sea_or_land = jnp.where(land, 1, 0)
    hot = jnp.where((mask_row == sea_or_land) & (lax.broadcasted_iota(jnp.int32, (16, LANES), 1) < NLON), 1.0, 0.0)
    xs[0, 192:208, :] = hot.astype(BF)
    xs[1, 192:208, :] = hot.astype(BF)
    bias_row = lax.broadcasted_iota(jnp.int32, (8, 384), 0)
    both = jnp.where(bias_row == 0, bv[0:1, :], jnp.where(bias_row == 1, bv[1:2, :], 0.0))
    bmat[...] = lax.dot_general(both, hot[0:8], (((0,), (0,)), ((), ())), precision=HIGH, preferred_element_type=F32)
    w_in_t[...] = w_in[...].T
    w_mid_t[...] = w_mid[...].T
    w_out[...] = w_out_t[...].T
    surf0, sbar0 = flat[0:1, :], flat[1:2, :]

    done(ra.at[pl.ds(0, 7)], 1)
    for g in range(GROUP):
        u, v, t, _ = unpack(ra[g].astype(F32))
        for f, part in enumerate((u, v, t)):
            st[f * 64 + g * 8 : f * 64 + g * 8 + 8, :] = part
    hgt[...] = falling(weight * st[128:192, :]) + surf0
    halo_send(0, st[64:128, :], hgt[...])
    xs[0, 0:192, :] = st[...].astype(BF)
    tend = forward(0)

    done(rb.at[pl.ds(0, 7)], 3)
    for g in range(GROUP):
        u, v, t, _ = unpack(rb[g].astype(F32))
        for f, part in enumerate((u, v, t)):
            br[f * 64 + g * 8 : f * 64 + g * 8 + 8, :] = part
    dbr[...] = div_bar(sbar0)
    halo_send(1, br[64:128, :], dbr[...])

    du, dv, dt, dsurf = dynamics(*halo_take(0))
    for i, d in enumerate((du, dv, dt)):
        at = slice(64 * i, 64 * i + 64)
        change = TIME_STEP * (d + tend[at])
        inc[at, :] = change
        st[at, :] = st[at, :] + change
    surf_inc = TIME_STEP * dsurf
    surf1 = surf0 + surf_inc
    hgt[...] = falling(weight * st[128:192, :]) + surf1
    halo_send(2, st[64:128, :], hgt[...])
    xs[1, 0:192, :] = st[...].astype(BF)
    tend = forward(1)

    t0 = br[...].astype(BF)
    second_bar, first_bar, input_bar = backward(1, t0)
    au, av, at_, asurf = adjoint(*halo_take(1))
    for i, d in enumerate((au, av, at_)):
        at = slice(64 * i, 64 * i + 64)
        change = d + input_bar[at]
        ginc[at, :] = change
        br[at, :] = jnp.where(real, br[at, :] + TIME_STEP * change, 0.0)
    gsurf = asurf
    sbar1 = sbar0 + TIME_STEP * asurf
    dbr[...] = div_bar(sbar1)
    halo_send(3, br[64:128, :], dbr[...])

    du, dv, dt, dsurf = dynamics(*halo_take(2))
    for i, d in enumerate((du, dv, dt)):
        at = slice(64 * i, 64 * i + 64)
        inc[at, :] = inc[at, :] + TIME_STEP * (d + tend[at])
    lay_out(f_s, inc, surf_inc + TIME_STEP * dsurf, f_r)
    give(f_s, f_r, 2)

    for at, g in gradients(1, t0, second_bar, first_bar):
        gacc[at : at + g.shape[0], :] = g

    def share(ref, q, part):
        return ref.at[pl.ds(pl.multiple_of(q * SHARE[part], 16), SHARE[part])]

    def stage(total, at, part):
        for b in range(3):
            base = PART[part] * b + at
            gs[part][base : base + total.shape[0], :] = total[:, 128 * b : 128 * b + 128].astype(BF)

    def scatter(part):
        rows = 16 * SHARE[part]
        push(gs[part].at[pl.ds(pl.multiple_of((1 - core) * rows, 16), rows)], mr[part], 4 + part, mate)

    def combine(part):
        done(mr[part], 2 * (4 + part) + 1)
        rows = 16 * SHARE[part]
        own = gs[part][pl.ds(pl.multiple_of(core * rows, 16), rows), :].astype(F32)
        cs[part][...] = (own + mr[part][...].astype(F32)).astype(BF)
        each(16, me_c, lambda q: push(share(cs[part], q, part), gr[part].at[me_c], 14 + part, of_plane(core * 16 + q)))

    gs1[3 * PART[1] :, :] = jnp.zeros((PLANE * SHARE[1] - 3 * PART[1], 128), BF)
    t1 = br[...].astype(BF)
    second_bar = (dot(w_out[...], t1) * s2[0]).astype(BF)
    stage(gacc[0:192, :] + dot_last(t1, a2[0]), 0, 0)
    mid = gacc[192:576, :] + dot_last(a1[0], second_bar)
    stage(mid[0:320], 192, 0)
    stage(mid[320:384], 0, 1)
    scatter(0)
    first_bar = (dot(w_mid[...], second_bar) * s1[0]).astype(BF)
    stage(gacc[576:784, :] + dot_last(xs[0], first_bar), 64, 1)
    scatter(1)
    combine(0)
    input_bar = dot(w_in[...], first_bar).astype(BF).astype(F32)
    combine(1)

    au, av, at_, asurf = adjoint(*halo_take(3))
    for i, d in enumerate((au, av, at_)):
        at = slice(64 * i, 64 * i + 64)
        ginc[at, :] = ginc[at, :] + d + input_bar[at]
    lay_out(o_s, ginc, gsurf + asurf, o_r)

    def sum_plane(part):
        done(gr[part].at[pl.ds(0, 15)], 2 * (14 + part) + 1)
        mine = cs[part][pl.ds(pl.multiple_of(me_c * SHARE[part], 16), SHARE[part]), :].astype(F32)
        near[part][pos] = lax.fori_loop(
            1, 16, lambda p, acc: acc + gr[part][lax.rem(me_c + p, 16)].astype(F32), mine
        )
        each(4, pos, lambda q: push(near[part].at[pos], near[part].at[pos], 6 + part, of_near(q)))

    def sum_near(part):
        done(near[part].at[pl.ds(0, 3)], 2 * (6 + part) + 1)
        n = near[part]
        far[part][me_f] = (n[0] + n[1]) + (n[2] + n[3])
        each(4, me_f, lambda q: push(far[part].at[me_f], far[part].at[me_f], 8 + part, of_far(q)))

    def sum_far(part):
        done(far[part].at[pl.ds(0, 3)], 2 * (8 + part) + 1)
        f = far[part]
        at = pl.ds(pl.multiple_of(me_p * SHARE[part], 16), SHARE[part])
        ag[part][at, :] = ((f[0] + f[1]) + (f[2] + f[3])).astype(BF)
        own = share(ag[part], me_p, part)
        each(16, me_c, lambda q: push(own, own, 10 + part, of_plane(core * 16 + q)))

    def to_mate(part):
        done(ag[part].at[pl.ds(0, 15 * SHARE[part])], 2 * (10 + part) + 1)
        rows = 16 * SHARE[part]
        half = ag[part].at[pl.ds(pl.multiple_of(core * rows, 16), rows)]
        push(half, half, 12 + part, mate)

    sum_plane(0)
    sum_plane(1)
    sum_near(0)
    sum_near(1)
    give(o_s, o_r, 3)
    def columns_out(came, out):
        for g in range(GROUP):
            u, v, t, rest = unpack(came[g].astype(F32))
            high = jnp.concatenate([rest[0:1], rest[1:2], rest[2:3]], axis=1)
            low = jnp.concatenate([rest[3:4], rest[4:5], rest[5:6]], axis=1)
            row = lax.broadcasted_iota(jnp.int32, (8, LANES), 0)
            tail = jnp.where(row == 0, high, jnp.where(row == 1, low, 0.0))
            out[g] = jnp.concatenate([u, v, t, tail], axis=0).astype(BF)

    done(f_r.at[pl.ds(0, 7)], 5)
    columns_out(f_r, out_f)
    sum_far(0)
    sum_far(1)

    to_mate(0)
    to_mate(1)

    def taken_from(part, b, first, last):
        base = PART[part] * b
        return ag[part][base + first : base + last, :]

    done(ag0.at[pl.ds(0, 16 * SHARE[0])], 25)
    for b in range(3):
        lanes = slice(128 * b, 128 * b + 128)
        g_out[:, lanes] = taken_from(0, b, 0, 192)
        g_mid[0:320, lanes] = taken_from(0, b, 192, 512)
    done(ag1.at[pl.ds(0, 16 * SHARE[1])], 27)
    for b in range(3):
        lanes = slice(128 * b, 128 * b + 128)
        g_mid[320:384, lanes] = taken_from(1, b, 0, 64)
        g_in[:, lanes] = taken_from(1, b, 64, 256)
        g_bias[:, lanes] = taken_from(1, b, 256, 272)
    done(o_r.at[pl.ds(0, 7)], 7)
    columns_out(o_r, out_g)
    leave()


def call(*operands):
    def v(shape, dtype):
        return pltpu.VMEM(shape, dtype)

    slab = (GROUP, *SLAB)
    hidden = (2, 384, LANES)
    hbm, vmem = pl.BlockSpec(memory_space=pl.ANY), pl.BlockSpec(memory_space=pltpu.VMEM)
    return pl.pallas_call(
        kernel,
        out_shape=(
            jax.ShapeDtypeStruct((GROUP, 32, LANES), BF),
            jax.ShapeDtypeStruct((GROUP, 32, LANES), BF),
            jax.ShapeDtypeStruct((192, 384), BF),
            jax.ShapeDtypeStruct((384, 384), BF),
            jax.ShapeDtypeStruct((192, 384), BF),
            jax.ShapeDtypeStruct((16, 384), BF),
        ),
        in_specs=[vmem] * 2 + [hbm] * 7,
        out_specs=tuple([vmem] * 6),
        scratch_shapes=[
            v((192, 384), BF), v((384, 384), BF), v((384, 192), BF),
            v((384, 192), BF), v((384, 384), BF), v((192, 384), BF),
            v((2, NLON), F32), v((2, NLON), F32), v((2, NLON), jnp.int32), v((2, 384), F32),
            v((8, LANES), F32), v((384, LANES), F32),
            v((384, LANES), F32), v((64, LANES), F32), v((64, LANES), F32),
            v(slab, BF), v(slab, BF), v(slab, BF), v(slab, BF),
            v((4, 128, LANES), BF), v((4, 2, 128, LANES), BF),
            v((192, LANES), F32), v((192, LANES), F32), v((2, 208, LANES), BF),
            v(hidden, BF), v(hidden, BF), v(hidden, F32), v(hidden, F32),
            v((192, LANES), F32), v((192, LANES), F32),
            v(slab, BF), v(slab, BF), v(slab, BF), v(slab, BF),
            v((GROWS, 384), F32),
            v((PLANE * SHARE[0], 128), BF), v((PLANE * SHARE[1], 128), BF),
            v((16 * SHARE[0], 128), BF), v((16 * SHARE[1], 128), BF),
            v((16 * SHARE[0], 128), BF), v((16 * SHARE[1], 128), BF),
            v((16, SHARE[0], 128), BF), v((16, SHARE[1], 128), BF),
            v((4, SHARE[0], 128), F32), v((4, SHARE[1], 128), F32),
            v((4, SHARE[0], 128), F32), v((4, SHARE[1], 128), F32),
            v((PLANE * SHARE[0], 128), BF), v((PLANE * SHARE[1], 128), BF),
            pltpu.SemaphoreType.DMA((32,)), pltpu.SemaphoreType.DMA((4, 2, 2)), pltpu.SemaphoreType.DMA((7,)),
        ],
        compiler_params=pltpu.CompilerParams(
            collective_id=0, has_side_effects=True, vmem_limit_bytes=24 * 2**20
        ),
        name="window",
    )(*operands)


def on_device(fields, surface, cot_fields, cot_surface, land_sea, w_in, w_mid, w_out, bias_in):
    lev_i, tile_i = lax.axis_index("lev"), lax.axis_index("tile")
    row = tile_i * 2 + row_of(lev_i, tile_i)
    latitude = -0.5 * math.pi + (row.astype(F32) + 0.5) * (math.pi / (2 * TILES))
    x_factor = 0.5 / jnp.maximum(jnp.cos(latitude), COS_FLOOR)
    sin_lat = jnp.sin(latitude)

    def pad(values):
        return jnp.pad(values, [(0, 0)] * (values.ndim - 1) + [(0, LANES - NLON)])

    def to_columns(values):
        split = values.astype(BF).reshape(3, 8, 2, 2, 2, NLON)
        return pad(split.transpose(2, 4, 3, 0, 1, 5).reshape(8, 24, NLON))

    sent = jnp.concatenate([to_columns(fields), to_columns(TIME_STEP * cot_fields)], axis=1)
    consts = jnp.stack([x_factor, sin_lat, (row > 0).astype(F32), (row < 2 * TILES - 1).astype(F32)])
    consts = jnp.broadcast_to(jnp.concatenate([consts, consts])[:, None], (8, LANES))
    came_f, came_g, g_in, g_mid, g_out, g_bias = call(
        sent, consts, surface, cot_surface, land_sea, bias_in, w_in, w_mid, w_out.T
    )

    def returned(came):
        came = came[:, :, :NLON].astype(F32)
        levels = came[:, :24].reshape(2, 2, 2, 3, 8, NLON).transpose(3, 4, 0, 2, 1, 5).reshape(3, 8, 4, 2, NLON)
        level_flat = (came[:, 24] + came[:, 25]).reshape(2, 2, 2, NLON).transpose(0, 2, 1, 3).reshape(4, 2, NLON)
        return levels, level_flat

    df, ds = returned(came_f)
    dg, dgs = returned(came_g)
    return (
        fields + df,
        surface + ds,
        cot_fields + dg,
        cot_surface + dgs,
        g_in.astype(F32),
        g_mid.astype(F32),
        g_out.T.astype(F32),
        g_bias[:2].astype(F32),
    )


def solution(mesh):
    levels = P(None, ("lev", "sec"), None, "tile", None)
    flat = P(None, "tile", None)
    return jax.shard_map(
        on_device,
        mesh=mesh,
        in_specs=(levels, flat, levels, flat, P("tile", None), P(), P(), P(), P()),
        out_specs=(levels, flat, levels, flat, P(), P(), P(), P()),
        check_vma=False,
    )
```

```python
import functools
import math

import jax
import jax.numpy as jnp
from jax import lax
from jax.experimental import pallas as pl
from jax.experimental.pallas import tpu as pltpu
from jax.sharding import PartitionSpec as P

TIME_STEP = 0.1
COS_FLOOR = 0.2
INV_SQRT_TWO = 1.0 / math.sqrt(2.0)
INV_SQRT_TWO_PI = 1.0 / math.sqrt(2.0 * math.pi)
EVERY = ("lev", "tile", "sec")
HIGH = lax.Precision.HIGHEST
MESH = pl.DeviceIdType.MESH
BF = jnp.bfloat16
F32 = jnp.float32
NLEV, NLON, LANES = 64, 360, 384
TILES, GROUP, PLANE = 64, 8, 32
GROWS = 784
PART = (512, 272)
SHARE = (48, 32)
SLAB = (16, 640)


def dot(a, b):
    return jnp.dot(a, b, preferred_element_type=F32)


def dot_last(a, b):
    return lax.dot_general(a, b, (((1,), (1,)), ((), ())), preferred_element_type=F32)


def row_of(lev, tile):
    return lax.rem(lev + lax.rem(tile, 2), 2)


def sample_half(lev, tile):
    flip = lax.rem(tile, 2) * (1 - lax.rem(lev, 2))
    return lax.rem(lax.div(lev, 2) + lax.rem(lax.div(tile, 2), 2) + flip, 2)


def kernel(
    sent, consts, surface, cot_surface, land_sea, bias, w_in_h, w_mid_h, w_out_h,
    out_f, out_g, g_in, g_mid, g_out, g_bias,
    w_in, w_mid, w_out, w_in_t, w_mid_t, w_out_t, sv, cv, mv, bv, flat, bmat,
    pre, hgt, dbr, a_s, b_s, ra, rb, hs, hr, st, br, xs, a1, a2, s1, s2, inc, ginc,
    f_s, f_r, o_s, o_r, gacc, gs0, gs1, mr0, mr1, cs0, cs1, gr0, gr1, near0, near1, far0, far1, ag0, ag1,
    sems, hsem, wsem,
):
    lev, tile, sec = (lax.axis_index(a) for a in EVERY)
    r = row_of(lev, tile)
    me_g = lev * 2 + sec
    spot = lax.rem(tile, 8)
    z_lo = lax.div(tile, 8)
    core = lax.rem(spot, 2)
    me_c = lev * 4 + lax.div(spot, 2)
    me_p = core * 16 + me_c
    mate = (lev, tile + 1 - 2 * core, sec)
    pos = lax.rem(z_lo, 4)
    quad = lax.div(z_lo, 4)
    me_f = sec * 2 + quad
    half_of = sample_half(lev, tile)
    sample = half_of * 2 + sec
    my_slot = (half_of * 2 + r) * 2 + sec
    gs, mr, cs, gr, near, far, ag = (gs0, gs1), (mr0, mr1), (cs0, cs1), (gr0, gr1), (near0, near1), (far0, far1), (ag0, ag1)

    def of_group(q):
        return (lax.div(q, 2), tile, lax.rem(q, 2))

    def of_plane(q):
        chip = lax.rem(q, 16)
        return (lax.div(chip, 4), z_lo * 8 + lax.rem(chip, 4) * 2 + lax.div(q, 16), sec)

    def of_near(q):
        return (lev, (quad * 4 + q) * 8 + spot, sec)

    def of_far(q):
        return (lev, (lax.rem(q, 2) * 4 + pos) * 8 + spot, lax.div(q, 2))

    def slot(q):
        their = lax.div(q, 2)
        return (sample_half(their, tile) * 2 + row_of(their, tile)) * 2 + lax.rem(q, 2)

    partner = lax.rem(lev + 5 - 2 * r, 4)
    above = (lev + (1 - r) * (partner - lev), lax.rem(tile + r, TILES), sec)
    below_dev = (lev + r * (partner - lev), lax.rem(tile + TILES - 1 + r, TILES), sec)

    fetches = [
        pltpu.make_async_copy(src, dst, wsem.at[i])
        for i, (src, dst) in enumerate(
            (
                (surface.at[sample], sv), (cot_surface.at[sample], cv), (land_sea, mv), (bias, bv),
                (w_in_h, w_in), (w_mid_h, w_mid), (w_out_h, w_out_t),
            )
        )
    ]
    for copy in fetches:
        copy.start()

    barrier = pltpu.get_barrier_semaphore()

    def greet(where):
        pl.semaphore_signal(barrier, inc=1, device_id=where, device_id_type=MESH)

    def each(n, me, act):
        def go(p, c):
            act(lax.rem(me + p, n))
            return c

        lax.fori_loop(1, n, go, 0)

    each(GROUP, me_g, lambda q: greet(of_group(q)))
    greet(above)
    greet(below_dev)
    each(16, me_c, lambda q: greet(of_plane(core * 16 + q)))
    greet(mate)
    each(4, pos, lambda q: greet(of_near(q)))
    each(4, me_f, lambda q: greet(of_far(q)))

    def pack(dst, g, uv, t, rest):
        dst[g, :, 0:384] = uv.astype(BF)
        dst[g, :, 384:512] = jnp.concatenate([t[:, 0:128], t[:, 256:384]], axis=0).astype(BF)
        dst[g, :, 512:640] = jnp.concatenate([t[:, 128:256], rest], axis=0).astype(BF)

    def unpack(slab):
        uv, one, two = slab[:, 0:384], slab[:, 384:512], slab[:, 512:640]
        t = jnp.concatenate([one[0:8], two[0:8], one[8:16]], axis=1)
        return uv[0:8], uv[8:16], t, two[8:16]

    nothing = jnp.zeros((8, 128), F32)
    for g in range(GROUP):
        for base, dst in ((0, a_s), (24, b_s)):
            wide = sent[g, base : base + 24, :].astype(F32)
            pack(dst, g, wide[0:16], wide[16:24], nothing)
    pl.semaphore_wait(barrier, GROUP - 1 + 2 + 15 + 1 + 3 + 3)

    def push(src, dst, k, where):
        pushed.add(k)
        pltpu.make_async_remote_copy(
            src_ref=src, dst_ref=dst, send_sem=sems.at[2 * k], recv_sem=sems.at[2 * k + 1],
            device_id=where, device_id_type=MESH,
        ).start()

    def finish(ref, sem):
        pltpu.make_async_copy(ref, ref, sem).wait()

    pushed, taken, halos_sent, halos_taken = set(), set(), set(), set()

    def done(ref, i):
        taken.add(i)
        finish(ref, sems.at[i])

    def leave():
        sizes = (
            ra.at[pl.ds(0, 7)], rb.at[pl.ds(0, 7)], f_r.at[pl.ds(0, 7)], o_r.at[pl.ds(0, 7)],
            mr0, mr1, near0.at[pl.ds(0, 3)], near1.at[pl.ds(0, 3)],
            far0.at[pl.ds(0, 3)], far1.at[pl.ds(0, 3)],
            ag0.at[pl.ds(0, 15 * SHARE[0])], ag1.at[pl.ds(0, 15 * SHARE[1])],
            ag0.at[pl.ds(0, 16 * SHARE[0])], ag1.at[pl.ds(0, 16 * SHARE[1])],
            gr0.at[pl.ds(0, 15)], gr1.at[pl.ds(0, 15)],
        )
        for k in sorted(pushed):
            done(sizes[k], 2 * k)
            if 2 * k + 1 not in taken:
                done(sizes[k], 2 * k + 1)
        for k in sorted(halos_sent):
            for way in (0, 1):
                finish(hs.at[k], hsem.at[k, way, 0])
                if k not in halos_taken:
                    finish(hr.at[k, way], hsem.at[k, way, 1])

    each(GROUP, me_g, lambda q: push(a_s.at[slot(q)], ra.at[me_g], 0, of_group(q)))
    each(GROUP, me_g, lambda q: push(b_s.at[slot(q)], rb.at[me_g], 1, of_group(q)))

    lane = lax.broadcasted_iota(jnp.int32, (64, LANES), 1)
    real = lane < NLON
    level = lax.broadcasted_iota(jnp.int32, (64, LANES), 0).astype(F32)
    weight = 1.0 / (level + 1.0)
    row_i = lax.broadcasted_iota(jnp.int32, (64, 192), 0)
    col_i = lax.broadcasted_iota(jnp.int32, (64, 192), 1)
    col_i = jnp.where(col_i >= 128, col_i - 128, jnp.where(col_i >= 64, col_i - 64, col_i))
    tri_rise = jnp.where(row_i >= col_i, 1.0, 0.0).astype(BF)
    tri_fall = jnp.where(row_i <= col_i, 1.0, 0.0).astype(BF)
    x_factor, sin_lat = consts[0:1, :], consts[1:2, :]
    has_before, has_after = consts[2:3, :] > 0, consts[3:4, :] > 0

    def vertical(which, values):
        one = values.astype(BF)
        rest = values - one.astype(F32)
        two = rest.astype(BF)
        three = (rest - two.astype(F32)).astype(BF)
        return dot(which, jnp.concatenate([one, two, three], axis=0))

    def rising(values):
        return vertical(tri_rise, values)

    def falling(values):
        return vertical(tri_fall, values)

    def dx(values):
        rows = values.shape[0]
        ln = lax.broadcasted_iota(jnp.int32, (rows, LANES), 1)
        full = jnp.where(ln == NLON, pltpu.roll(values, NLON, 1), values)
        full = jnp.where(ln == LANES - 1, pltpu.roll(values, LANES - NLON, 1), full)
        return (pltpu.roll(full, LANES - 1, 1) - pltpu.roll(full, 1, 1)) * x_factor

    def halo_send(k, first, second):
        halos_sent.add(k)
        hs[k, 0:64, :] = first.astype(BF)
        hs[k, 64:128, :] = second.astype(BF)
        for way, where in ((0, above), (1, below_dev)):
            pltpu.make_async_remote_copy(
                src_ref=hs.at[k], dst_ref=hr.at[k, way], send_sem=hsem.at[k, way, 0],
                recv_sem=hsem.at[k, way, 1], device_id=where, device_id_type=MESH,
            ).start()

    def halo_take(k):
        halos_taken.add(k)
        for way in (0, 1):
            finish(hr.at[k, way], hsem.at[k, way, 1])
        before, after = hr[k, 0].astype(F32), hr[k, 1].astype(F32)
        zero = jnp.zeros((), F32)
        diff = (jnp.where(has_after, after, zero) - jnp.where(has_before, before, zero)) * 0.5
        return diff[0:64], diff[64:128]

    def forward(k):
        pre[...] = dot(w_in_t[...], xs[k, 0:192, :])
        keep(a1, s1, k, True)
        pre[...] = dot(w_mid_t[...], a1[k])
        keep(a2, s2, k, False)
        return dot(w_out_t[...], a2[k]).astype(BF).astype(F32)

    def keep(act, slope, k, biased):
        def block(i, c):
            rows = pl.ds(pl.multiple_of(i * 32, 32), 32)
            value = pre[rows, :] + bmat[rows, :] if biased else pre[rows, :]
            cumulative = 0.5 * (1.0 + lax.erf(value * INV_SQRT_TWO))
            density = jnp.exp(-0.5 * value * value) * INV_SQRT_TWO_PI
            act[k, rows, :] = (value * cumulative).astype(BF)
            slope[k, rows, :] = cumulative + value * density
            return c

        lax.fori_loop(0, 12, block, 0)

    def backward(k, tend_bar):
        second_bar = (dot(w_out[...], tend_bar) * s2[k]).astype(BF)
        first_bar = (dot(w_mid[...], second_bar) * s1[k]).astype(BF)
        return second_bar, first_bar, dot(w_in[...], first_bar).astype(BF).astype(F32)

    def gradients(k, tend_bar, second_bar, first_bar):
        return (
            (0, dot_last(tend_bar, a2[k])),
            (192, dot_last(a1[k], second_bar)),
            (576, dot_last(xs[k], first_bar)),
        )

    def dynamics(dv, dh):
        u, v = st[0:64, :], st[64:128, :]
        div = dx(u) + dv
        flux = rising(div) * (1.0 / NLEV)
        return (
            -dx(hgt[...]) + sin_lat * v, -dh - sin_lat * u, -flux,
            jnp.sum(div, axis=0, keepdims=True) * (-1.0 / NLEV),
        )

    def div_bar(surf_bar):
        return (-falling(br[128:192, :]) - surf_bar) * (1.0 / NLEV)

    def adjoint(da, ddb):
        a_u, a_v = br[0:64, :], br[64:128, :]
        hb = dx(a_u) + da
        return (
            -dx(dbr[...]) - sin_lat * a_v, -ddb + sin_lat * a_u, weight * rising(hb),
            jnp.sum(hb, axis=0, keepdims=True),
        )

    def give(src, change, surf_change, dst, k):
        high = surf_change.astype(BF)
        low = (surf_change - high.astype(F32)).astype(BF)
        rows = lax.broadcasted_iota(jnp.int32, (8, 128), 0)
        tail = nothing
        for i in range(6):
            block = (high, low)[i // 3].astype(F32)[:, 128 * (i % 3) : 128 * (i % 3) + 128]
            tail = jnp.where(rows == i, block, tail)
        for g in range(GROUP):
            u, v, t = (change[f * 64 + g * 8 : f * 64 + g * 8 + 8, :] for f in range(3))
            pack(src, g, jnp.concatenate([u, v], axis=0), t, tail)
        dst[my_slot] = src[me_g]
        each(GROUP, me_g, lambda q: push(src.at[q], dst.at[my_slot], k, of_group(q)))

    ra[me_g] = a_s[my_slot]
    rb[me_g] = b_s[my_slot]
    for copy in fetches:
        copy.wait()
    flat[...] = jnp.zeros_like(flat)
    flat[0:1, 0:NLON] = jnp.where(r == 0, sv[0:1, :], sv[1:2, :])
    flat[1:2, 0:NLON] = TIME_STEP * jnp.where(r == 0, cv[0:1, :], cv[1:2, :])
    flat[2:3, 0:NLON] = jnp.where(jnp.where(r == 0, mv[0:1, :], mv[1:2, :]) > 0, 1.0, 0.0)
    land = flat[2:3, :] > 0
    mask_row = lax.broadcasted_iota(jnp.int32, (16, LANES), 0)
    sea_or_land = jnp.where(land, 1, 0)
    hot = jnp.where((mask_row == sea_or_land) & (lax.broadcasted_iota(jnp.int32, (16, LANES), 1) < NLON), 1.0, 0.0)
    xs[0, 192:208, :] = hot.astype(BF)
    xs[1, 192:208, :] = hot.astype(BF)
    bias_row = lax.broadcasted_iota(jnp.int32, (8, 384), 0)
    both = jnp.where(bias_row == 0, bv[0:1, :], jnp.where(bias_row == 1, bv[1:2, :], 0.0))
    bmat[...] = lax.dot_general(both, hot[0:8], (((0,), (0,)), ((), ())), precision=HIGH, preferred_element_type=F32)
    w_in_t[...] = w_in[...].T
    w_mid_t[...] = w_mid[...].T
    w_out[...] = w_out_t[...].T
    surf0, sbar0 = flat[0:1, :], flat[1:2, :]

    done(ra.at[pl.ds(0, 7)], 1)
    for g in range(GROUP):
        u, v, t, _ = unpack(ra[g].astype(F32))
        for f, part in enumerate((u, v, t)):
            st[f * 64 + g * 8 : f * 64 + g * 8 + 8, :] = part
    hgt[...] = falling(weight * st[128:192, :]) + surf0
    halo_send(0, st[64:128, :], hgt[...])
    xs[0, 0:192, :] = st[...].astype(BF)
    tend = forward(0)

    done(rb.at[pl.ds(0, 7)], 3)
    for g in range(GROUP):
        u, v, t, _ = unpack(rb[g].astype(F32))
        for f, part in enumerate((u, v, t)):
            br[f * 64 + g * 8 : f * 64 + g * 8 + 8, :] = part
    dbr[...] = div_bar(sbar0)
    halo_send(1, br[64:128, :], dbr[...])

    du, dv, dt, dsurf = dynamics(*halo_take(0))
    for i, d in enumerate((du, dv, dt)):
        at = slice(64 * i, 64 * i + 64)
        change = TIME_STEP * (d + tend[at])
        inc[at, :] = change
        st[at, :] = st[at, :] + change
    surf_inc = TIME_STEP * dsurf
    surf1 = surf0 + surf_inc
    hgt[...] = falling(weight * st[128:192, :]) + surf1
    halo_send(2, st[64:128, :], hgt[...])
    xs[1, 0:192, :] = st[...].astype(BF)
    tend = forward(1)

    t0 = br[...].astype(BF)
    second_bar, first_bar, input_bar = backward(1, t0)
    au, av, at_, asurf = adjoint(*halo_take(1))
    for i, d in enumerate((au, av, at_)):
        at = slice(64 * i, 64 * i + 64)
        change = d + input_bar[at]
        ginc[at, :] = change
        br[at, :] = jnp.where(real, br[at, :] + TIME_STEP * change, 0.0)
    gsurf = asurf
    sbar1 = sbar0 + TIME_STEP * asurf
    dbr[...] = div_bar(sbar1)
    halo_send(3, br[64:128, :], dbr[...])

    for at, g in gradients(1, t0, second_bar, first_bar):
        gacc[at : at + g.shape[0], :] = g

    def share(ref, q, part):
        return ref.at[pl.ds(pl.multiple_of(q * SHARE[part], 16), SHARE[part])]

    def stage(total, at, part):
        for b in range(3):
            base = PART[part] * b + at
            gs[part][base : base + total.shape[0], :] = total[:, 128 * b : 128 * b + 128].astype(BF)

    def scatter(part):
        rows = 16 * SHARE[part]
        push(gs[part].at[pl.ds(pl.multiple_of((1 - core) * rows, 16), rows)], mr[part], 4 + part, mate)

    def combine(part):
        done(mr[part], 2 * (4 + part) + 1)
        rows = 16 * SHARE[part]
        own = gs[part][pl.ds(pl.multiple_of(core * rows, 16), rows), :].astype(F32)
        cs[part][...] = (own + mr[part][...].astype(F32)).astype(BF)
        each(16, me_c, lambda q: push(share(cs[part], q, part), gr[part].at[me_c], 14 + part, of_plane(core * 16 + q)))

    gs1[3 * PART[1] :, :] = jnp.zeros((PLANE * SHARE[1] - 3 * PART[1], 128), BF)
    t1 = br[...].astype(BF)
    second_bar = (dot(w_out[...], t1) * s2[0]).astype(BF)
    stage(gacc[0:192, :] + dot_last(t1, a2[0]), 0, 0)
    mid = gacc[192:576, :] + dot_last(a1[0], second_bar)
    stage(mid[0:320], 192, 0)
    stage(mid[320:384], 0, 1)
    scatter(0)
    first_bar = (dot(w_mid[...], second_bar) * s1[0]).astype(BF)
    stage(gacc[576:784, :] + dot_last(xs[0], first_bar), 64, 1)
    scatter(1)
    combine(0)
    input_bar = dot(w_in[...], first_bar).astype(BF).astype(F32)
    combine(1)

    au, av, at_, asurf = adjoint(*halo_take(3))
    for i, d in enumerate((au, av, at_)):
        at = slice(64 * i, 64 * i + 64)
        ginc[at, :] = ginc[at, :] + d + input_bar[at]
    give(o_s, ginc, gsurf + asurf, o_r, 3)

    du, dv, dt, dsurf = dynamics(*halo_take(2))
    for i, d in enumerate((du, dv, dt)):
        at = slice(64 * i, 64 * i + 64)
        inc[at, :] = inc[at, :] + TIME_STEP * (d + tend[at])
    give(f_s, inc, surf_inc + TIME_STEP * dsurf, f_r, 2)


    def sum_plane(part):
        done(gr[part].at[pl.ds(0, 15)], 2 * (14 + part) + 1)
        mine = cs[part][pl.ds(pl.multiple_of(me_c * SHARE[part], 16), SHARE[part]), :].astype(F32)
        near[part][pos] = lax.fori_loop(
            1, 16, lambda p, acc: acc + gr[part][lax.rem(me_c + p, 16)].astype(F32), mine
        )
        each(4, pos, lambda q: push(near[part].at[pos], near[part].at[pos], 6 + part, of_near(q)))

    def sum_near(part):
        done(near[part].at[pl.ds(0, 3)], 2 * (6 + part) + 1)
        n = near[part]
        far[part][me_f] = (n[0] + n[1]) + (n[2] + n[3])
        each(4, me_f, lambda q: push(far[part].at[me_f], far[part].at[me_f], 8 + part, of_far(q)))

    def sum_far(part):
        done(far[part].at[pl.ds(0, 3)], 2 * (8 + part) + 1)
        f = far[part]
        at = pl.ds(pl.multiple_of(me_p * SHARE[part], 16), SHARE[part])
        ag[part][at, :] = ((f[0] + f[1]) + (f[2] + f[3])).astype(BF)
        own = share(ag[part], me_p, part)
        each(16, me_c, lambda q: push(own, own, 10 + part, of_plane(core * 16 + q)))

    def to_mate(part):
        done(ag[part].at[pl.ds(0, 15 * SHARE[part])], 2 * (10 + part) + 1)
        rows = 16 * SHARE[part]
        half = ag[part].at[pl.ds(pl.multiple_of(core * rows, 16), rows)]
        push(half, half, 12 + part, mate)

    sum_plane(0)
    sum_plane(1)
    sum_near(0)
    sum_near(1)
    sum_far(0)
    sum_far(1)

    def columns_out(came, out):
        for g in range(GROUP):
            u, v, t, rest = unpack(came[g].astype(F32))
            high = jnp.concatenate([rest[0:1], rest[1:2], rest[2:3]], axis=1)
            low = jnp.concatenate([rest[3:4], rest[4:5], rest[5:6]], axis=1)
            row = lax.broadcasted_iota(jnp.int32, (8, LANES), 0)
            tail = jnp.where(row == 0, high, jnp.where(row == 1, low, 0.0))
            out[g] = jnp.concatenate([u, v, t, tail], axis=0).astype(BF)

    to_mate(0)
    done(f_r.at[pl.ds(0, 7)], 5)
    columns_out(f_r, out_f)
    to_mate(1)
    done(o_r.at[pl.ds(0, 7)], 7)
    columns_out(o_r, out_g)

    def taken_from(part, b, first, last):
        base = PART[part] * b
        return ag[part][base + first : base + last, :]

    done(ag0.at[pl.ds(0, 16 * SHARE[0])], 25)
    for b in range(3):
        lanes = slice(128 * b, 128 * b + 128)
        g_out[:, lanes] = taken_from(0, b, 0, 192)
        g_mid[0:320, lanes] = taken_from(0, b, 192, 512)
    done(ag1.at[pl.ds(0, 16 * SHARE[1])], 27)
    for b in range(3):
        lanes = slice(128 * b, 128 * b + 128)
        g_mid[320:384, lanes] = taken_from(1, b, 0, 64)
        g_in[:, lanes] = taken_from(1, b, 64, 256)
        g_bias[:, lanes] = taken_from(1, b, 256, 272)
    leave()


def call(*operands):
    def v(shape, dtype):
        return pltpu.VMEM(shape, dtype)

    slab = (GROUP, *SLAB)
    hidden = (2, 384, LANES)
    hbm, vmem = pl.BlockSpec(memory_space=pl.ANY), pl.BlockSpec(memory_space=pltpu.VMEM)
    return pl.pallas_call(
        kernel,
        out_shape=(
            jax.ShapeDtypeStruct((GROUP, 32, LANES), BF),
            jax.ShapeDtypeStruct((GROUP, 32, LANES), BF),
            jax.ShapeDtypeStruct((192, 384), BF),
            jax.ShapeDtypeStruct((384, 384), BF),
            jax.ShapeDtypeStruct((192, 384), BF),
            jax.ShapeDtypeStruct((16, 384), BF),
        ),
        in_specs=[vmem] * 2 + [hbm] * 7,
        out_specs=tuple([vmem] * 6),
        scratch_shapes=[
            v((192, 384), BF), v((384, 384), BF), v((384, 192), BF),
            v((384, 192), BF), v((384, 384), BF), v((192, 384), BF),
            v((2, NLON), F32), v((2, NLON), F32), v((2, NLON), jnp.int32), v((2, 384), F32),
            v((8, LANES), F32), v((384, LANES), F32),
            v((384, LANES), F32), v((64, LANES), F32), v((64, LANES), F32),
            v(slab, BF), v(slab, BF), v(slab, BF), v(slab, BF),
            v((4, 128, LANES), BF), v((4, 2, 128, LANES), BF),
            v((192, LANES), F32), v((192, LANES), F32), v((2, 208, LANES), BF),
            v(hidden, BF), v(hidden, BF), v(hidden, F32), v(hidden, F32),
            v((192, LANES), F32), v((192, LANES), F32),
            v(slab, BF), v(slab, BF), v(slab, BF), v(slab, BF),
            v((GROWS, 384), F32),
            v((PLANE * SHARE[0], 128), BF), v((PLANE * SHARE[1], 128), BF),
            v((16 * SHARE[0], 128), BF), v((16 * SHARE[1], 128), BF),
            v((16 * SHARE[0], 128), BF), v((16 * SHARE[1], 128), BF),
            v((16, SHARE[0], 128), BF), v((16, SHARE[1], 128), BF),
            v((4, SHARE[0], 128), F32), v((4, SHARE[1], 128), F32),
            v((4, SHARE[0], 128), F32), v((4, SHARE[1], 128), F32),
            v((PLANE * SHARE[0], 128), BF), v((PLANE * SHARE[1], 128), BF),
            pltpu.SemaphoreType.DMA((32,)), pltpu.SemaphoreType.DMA((4, 2, 2)), pltpu.SemaphoreType.DMA((7,)),
        ],
        compiler_params=pltpu.CompilerParams(
            collective_id=0, has_side_effects=True, vmem_limit_bytes=40 * 2**20
        ),
        name="window",
    )(*operands)


def on_device(fields, surface, cot_fields, cot_surface, land_sea, w_in, w_mid, w_out, bias_in):
    lev_i, tile_i = lax.axis_index("lev"), lax.axis_index("tile")
    row = tile_i * 2 + row_of(lev_i, tile_i)
    latitude = -0.5 * math.pi + (row.astype(F32) + 0.5) * (math.pi / (2 * TILES))
    x_factor = 0.5 / jnp.maximum(jnp.cos(latitude), COS_FLOOR)
    sin_lat = jnp.sin(latitude)

    def pad(values):
        return jnp.pad(values, [(0, 0)] * (values.ndim - 1) + [(0, LANES - NLON)])

    def to_columns(values):
        split = values.astype(BF).reshape(3, 8, 2, 2, 2, NLON)
        return pad(split.transpose(2, 4, 3, 0, 1, 5).reshape(8, 24, NLON))

    sent = jnp.concatenate([to_columns(fields), to_columns(TIME_STEP * cot_fields)], axis=1)
    consts = jnp.stack([x_factor, sin_lat, (row > 0).astype(F32), (row < 2 * TILES - 1).astype(F32)])
    consts = jnp.broadcast_to(jnp.concatenate([consts, consts])[:, None], (8, LANES))
    came_f, came_g, g_in, g_mid, g_out, g_bias = call(
        sent, consts, surface, cot_surface, land_sea, bias_in, w_in, w_mid, w_out.T
    )

    def returned(came):
        came = came[:, :, :NLON].astype(F32)
        levels = came[:, :24].reshape(2, 2, 2, 3, 8, NLON).transpose(3, 4, 0, 2, 1, 5).reshape(3, 8, 4, 2, NLON)
        level_flat = (came[:, 24] + came[:, 25]).reshape(2, 2, 2, NLON).transpose(0, 2, 1, 3).reshape(4, 2, NLON)
        return levels, level_flat

    df, ds = returned(came_f)
    dg, dgs = returned(came_g)
    return (
        fields + df,
        surface + ds,
        cot_fields + dg,
        cot_surface + dgs,
        g_in.astype(F32),
        g_mid.astype(F32),
        g_out.T.astype(F32),
        g_bias[:2].astype(F32),
    )


def solution(mesh):
    levels = P(None, ("lev", "sec"), None, "tile", None)
    flat = P(None, "tile", None)
    return jax.shard_map(
        on_device,
        mesh=mesh,
        in_specs=(levels, flat, levels, flat, P("tile", None), P(), P(), P(), P()),
        out_specs=(levels, flat, levels, flat, P(), P(), P(), P()),
        check_vma=False,
    )
```
